32 devices in a mesh: energy: 8 (over y, x, core), momentum: 4 (over z).
Axes of the slice: x: 2, y: 2, z: 4, core: 2. Of those that a mesh axis runs over, the one named last changes fastest.
Arguments:
- green_blocks: float32 [2, 8, 4, 200, 256], P(None, 'energy', 'momentum'), may hold values from -6 to 6
- couple_matrix: float32 [3, 100, 256], P(None, None, ('energy', 'momentum')), may hold values from -1.8 to 1.8
- occupation: float32 [3], replicated, may hold values from 0.1 to 3
- energy_shift: int32 [3], replicated, may hold values from 1 to 7, as said below
- branch_weight: float32 [4, 3], replicated, may hold values from 0.3 to 3
- pair_branch: int32 [4, 4], replicated, may hold values from 0 to 3
Outputs:
- self_energy: float32 [2, 8, 4, 200, 256], P(None, 'energy', 'momentum')
The draws below stay inside these ranges and needn't reach their ends.
Inputs may be any that keep to these rules, and one draw needn't show every extreme that they name: `energy_shift`: the branches' shifts are distinct.
All inputs are finite; a program needn't handle non-finite values.
Results may differ from the reference program's by a relative error of at most 0.0001.
Values sent between devices are 32-bit elements; how exact they have to be, the bound alone decides.
A program may use at most 192 MiB of HBM per device.

```python
import math
import jax
import jax.numpy as jnp
from jax import lax

ORB = 10
MODES = 3
NE = 8
NK = 4
ATOMS = 256
NQ = 4


def draw_energy_shift(key, part):
    key = jax.random.fold_in(key, 11)
    first_key, second_key = jax.random.split(key)
    middle = jax.random.permutation(first_key, NE - 3)[:MODES - 2].astype(jnp.int32) + 2
    values = jnp.concatenate([jnp.array([1, NE - 1], dtype=jnp.int32), middle])
    order = jax.random.permutation(second_key, MODES)
    return values[order].astype(jnp.int32)


def place_ends(result, stream_key, low, top_value):
    extent = result.shape
    place = [jax.random.randint(jax.random.fold_in(stream_key, axis), (), 0, extent[axis]) for axis in range(len(extent))]
    result = result.at[tuple(place)].set(low)
    longest = extent.index(max(extent))
    place[longest] = (place[longest] + 1) % extent[longest]
    return result.at[tuple(place)].set(top_value)


def levels(stream_key, shape, shards, low, high):
    factor_of = 1.0
    for position, shards_of in shards:
        steps = jax.random.uniform(jax.random.fold_in(jax.random.fold_in(stream_key, 6), position), (shards_of,), jnp.float32, low / len(shards), high / len(shards))
        factor_of = factor_of * jnp.repeat(jnp.exp(steps), shape[position] // shards_of).reshape((-1,) + (1,) * (len(shape) - 1 - position))
    return factor_of


def bell_draw(rng, dims, deviation, limit, cuts=(), held_as=jnp.bfloat16):
    drawn = jax.random.normal(rng, dims, jnp.float32) * deviation
    if len(cuts) > 0:
        drawn = levels(rng, dims, cuts, -0.22, 0.18) * drawn
    return jnp.clip(drawn, min=-limit, max=limit).astype(held_as)


def setup_inputs(seed: int = 0) -> dict:
    keys = jax.random.split(jax.random.key(seed), 7)
    green_blocks = bell_draw(keys[0], (2, NE, NK, 2 * ORB * ORB, ATOMS), 1.0, 6.0, ((1, 8), (2, 4)), jnp.float32)
    couple_matrix = bell_draw(keys[1], (MODES, ORB * ORB, ATOMS), 0.3, 1.8, ((2, 32),), jnp.float32)
    occupation = jnp.clip(jnp.exp(jax.random.uniform(keys[2], (MODES,), jnp.float32, math.log(0.1), math.log(3.0))), 0.1, 3.0)
    energy_shift = draw_energy_shift(jax.random.fold_in(keys[6], 71), 0)
    branch_weight = jnp.clip(jnp.exp(jax.random.uniform(keys[4], (NQ, MODES), jnp.float32, math.log(0.3), math.log(3.0))), 0.3, 3.0)
    pair_branch = place_ends(jax.random.randint(keys[5], (NK, NK), 0, NQ), jax.random.fold_in(keys[5], 1), 0, NQ - 1).astype(jnp.int32)
    return dict(green_blocks=green_blocks, couple_matrix=couple_matrix, occupation=occupation, energy_shift=energy_shift, branch_weight=branch_weight, pair_branch=pair_branch)


def transform(field, couple, occupation, energy_shift, kind_index):
    energies = field.shape[0]
    momenta = field.shape[1]
    atoms_here = field.shape[3]
    padded = jnp.pad(field, ((energies, energies), (0, 0), (0, 0), (0, 0)))
    results = []
    for mode_index in range(couple.shape[0]):
        upper_part = lax.dynamic_slice_in_dim(padded, energies + energy_shift[mode_index], energies, 0)
        lower_part = lax.dynamic_slice_in_dim(padded, energies - energy_shift[mode_index], energies, 0)
        combined = (occupation[mode_index] + 1.0 - kind_index) * upper_part + (occupation[mode_index] + kind_index) * lower_part
        blocks = combined.reshape(energies, momenta, 2, ORB, ORB, atoms_here)
        coupling = couple[mode_index].reshape(ORB, ORB, atoms_here)
        left_product = jnp.einsum('ija,ekrjla->ekrila', coupling, blocks, precision=lax.Precision.HIGHEST)
        sandwich = jnp.einsum('ekrila,nla->ekrina', left_product, coupling, precision=lax.Precision.HIGHEST)
        results.append(sandwich.reshape(energies, momenta, 2 * ORB * ORB, atoms_here))
    return jnp.stack(results)


def mixing(branch_weight, pair_branch):
    onehot = (pair_branch[:, :, None] == jnp.arange(branch_weight.shape[0], dtype=jnp.int32)).astype(jnp.float32)
    return jnp.einsum('kjq,qm->mkj', onehot, branch_weight, precision=lax.Precision.HIGHEST)


def reference(green_blocks, couple_matrix, occupation, energy_shift, branch_weight, pair_branch):
    mixing_table = mixing(branch_weight, pair_branch) / NK
    results = []
    for kind_index in range(2):
        transformed = transform(green_blocks[kind_index], couple_matrix, occupation, energy_shift, kind_index)
        results.append(jnp.einsum('mkj,mejxa->ekxa', mixing_table, transformed, precision=lax.Precision.HIGHEST))
    return jnp.stack(results)
```

```python
import functools

import jax
import jax.numpy as jnp
from jax import lax
from jax.experimental import pallas as pl
from jax.experimental.pallas import tpu as pltpu
from jax.sharding import PartitionSpec as P

ORB = 10
PAIRS = ORB * ORB
LANES = 128
ROWS = 8
GROUP = 8
PIECES = LANES // GROUP
QUARTERS = 4
STEPS = PAIRS // QUARTERS
SLOT = 32
CHUNKS = SLOT // ROWS
MESH = pl.DeviceIdType.MESH


def swap_groups(arrays, lane, width):
    arrays = list(arrays)
    bit = 1
    while bit < len(arrays):
        low = ((lane // width) & bit) == 0
        for p in range(len(arrays)):
            if p & bit:
                continue
            a, b = arrays[p], arrays[p | bit]
            arrays[p] = jnp.where(low, a, pltpu.roll(b, bit * width, 1))
            arrays[p | bit] = jnp.where(low, pltpu.roll(a, LANES - bit * width, 1), b)
        bit *= 2
    return arrays


def total_of(terms):
    while len(terms) > 1:
        paired = [terms[i] + terms[i + 1] for i in range(0, len(terms) - 1, 2)]
        terms = paired + ([terms[-1]] if len(terms) % 2 else [])
    return terms[0]


def piece_rows(piece):
    quarter, kind, part = piece // 4, (piece // 2) % 2, piece % 2
    return kind * 2 * PAIRS + part * PAIRS + quarter


def kernel(
    n_energy,
    n_moment,
    modes,
    shift_ref,
    occupation_ref,
    weight_ref,
    branch_ref,
    couple_ref,
    green_ref,
    out_ref,
    inside,
    packed,
    arrived,
    mixed,
    coupling,
    coef,
    right_done,
    both_done,
    back,
    returned,
    outside,
    local_sem,
    send_sem,
    recv_sem,
    send_back_sem,
    recv_back_sem,
):
    count = n_energy * n_moment
    tiles = green_ref.shape[2] // LANES
    groups = n_moment // QUARTERS
    heights = n_energy // ROWS
    my_energy = lax.axis_index("energy")
    my_moment = lax.axis_index("momentum")

    def slot_of(energy, moment):
        return pl.multiple_of((moment * n_energy + energy) * SLOT, SLOT)

    def slot_of_rank(rank):
        return slot_of(rank // n_moment, rank % n_moment)

    def partner(offset, sign):
        energy = lax.rem(my_energy + sign * (offset // n_moment) + n_energy, n_energy)
        moment = lax.rem(my_moment + sign * (offset % n_moment) + n_moment, n_moment)
        return energy, moment

    loads = []
    for kind in range(2):
        for tile in range(tiles):
            load = pltpu.make_async_copy(
                green_ref.at[kind, :, pl.ds(tile * LANES, LANES)],
                inside.at[tile, pl.ds(kind * 2 * PAIRS, 2 * PAIRS)],
                local_sem.at[kind, tile],
            )
            load.start()
            loads.append(load)

    barrier = pltpu.get_barrier_semaphore()

    def greet(offset, carry):
        energy, moment = partner(offset, 1)
        pl.semaphore_signal(
            barrier, inc=1, device_id={"energy": energy, "momentum": moment}, device_id_type=MESH
        )
        return carry

    lax.fori_loop(1, count, greet, 0)

    lane = lax.broadcasted_iota(jnp.int32, (ROWS, LANES), 1)

    for load in loads:
        load.wait()

    def pack(tile, carry):
        for chunk in range(CHUNKS):
            pieces = [
                inside[
                    tile,
                    pl.ds(piece_rows(p) + QUARTERS * ROWS * chunk, ROWS, stride=QUARTERS),
                    :,
                ]
                for p in range(PIECES)
            ]
            for g, value in enumerate(swap_groups(pieces, lane, GROUP)):
                row = slot_of_rank(tile * PIECES + g) + chunk * ROWS
                packed[pl.ds(pl.multiple_of(row, ROWS), ROWS), :] = value
        return carry

    lax.fori_loop(0, tiles, pack, 0)

    pl.semaphore_wait(barrier, count - 1)

    mine = slot_of(my_energy, my_moment)

    def outgoing(source, target, sends, receives, offset):
        energy, moment = partner(offset, 1)
        return pltpu.make_async_remote_copy(
            src_ref=source.at[pl.ds(slot_of(energy, moment), STEPS)],
            dst_ref=target.at[pl.ds(mine, STEPS)],
            send_sem=sends.at[offset],
            recv_sem=receives.at[offset],
            device_id={"energy": energy, "momentum": moment},
            device_id_type=MESH,
        )

    def incoming(source, target, sends, receives, offset):
        energy, moment = partner(offset, -1)
        return pltpu.make_async_remote_copy(
            src_ref=source.at[pl.ds(mine, STEPS)],
            dst_ref=target.at[pl.ds(slot_of(energy, moment), STEPS)],
            send_sem=sends.at[offset],
            recv_sem=receives.at[offset],
            device_id={"energy": energy, "momentum": moment},
            device_id_type=MESH,
        )

    def exchange_start(source, target, sends, receives):
        def step(offset, carry):
            outgoing(source, target, sends, receives, offset).start()
            return carry

        lax.fori_loop(1, count, step, 0)
        own = pltpu.make_async_copy(
            source.at[pl.ds(mine, STEPS)], target.at[pl.ds(mine, STEPS)], receives.at[0]
        )
        own.start()
        return own

    def exchange_wait(source, target, sends, receives, own):
        def step(offset, carry):
            incoming(source, target, sends, receives, offset).wait_recv()
            return carry

        own.wait()
        lax.fori_loop(1, count, step, 0)

    def sends_wait(source, target, sends, receives):
        def step(offset, carry):
            outgoing(source, target, sends, receives, offset).wait_send()
            return carry

        lax.fori_loop(1, count, step, 0)

    there = (packed, arrived, send_sem, recv_sem)
    own = exchange_start(*there)

    spread = (
        lax.broadcasted_iota(jnp.int32, (GROUP, LANES), 1) % GROUP
        == lax.broadcasted_iota(jnp.int32, (GROUP, LANES), 0)
    ).astype(jnp.float32)
    for mode in range(modes):
        wide = jnp.dot(
            couple_ref[mode],
            spread,
            precision=lax.Precision.HIGHEST,
            preferred_element_type=jnp.float32,
        )
        coupling[pl.ds(mode * PAIRS, PAIRS)] = jnp.broadcast_to(
            wide[:, None, :], (PAIRS, ROWS, LANES)
        )

    lane_moment = lane // (LANES // QUARTERS)
    for mode in range(modes):
        for kg in range(groups):
            for jg in range(groups):
                for turn in range(QUARTERS):
                    value = jnp.zeros((ROWS, LANES), jnp.float32)
                    for kl in range(QUARTERS):
                        k = kg * QUARTERS + kl
                        j = jg * QUARTERS + (kl - turn) % QUARTERS
                        weight = weight_ref[branch_ref[k, j], mode] / n_moment
                        value = jnp.where(lane_moment == kl, weight, value)
                    coef[mode, kg, jg, turn] = value
    kind = ((lane // (2 * GROUP)) % 2).astype(jnp.float32)

    empty = jnp.zeros((n_energy, LANES), jnp.float32)
    for mode in range(modes):
        for kg in range(groups):

            def clear(pair, carry):
                row = pl.multiple_of(pair * 2 * n_energy, ROWS)
                mixed[mode, kg, pl.ds(row, n_energy), :] = empty
                return carry

            lax.fori_loop(0, PAIRS + 1, clear, 0)

    exchange_wait(*there, own)

    def mix_step(step, carry):
        for height in range(heights):
            quarters = []
            for jg in range(groups):
                values = [
                    arrived[
                        pl.ds(
                            ((jg * QUARTERS + jl) * n_energy + height * ROWS) * SLOT + step,
                            ROWS,
                            stride=SLOT,
                        ),
                        :,
                    ]
                    for jl in range(QUARTERS)
                ]
                quarters.append(swap_groups(values, lane, LANES // QUARTERS))
            for q in range(QUARTERS):
                turned = [
                    [quarters[jg][q]]
                    + [pltpu.roll(quarters[jg][q], turn * GROUP * 4, 1) for turn in range(1, QUARTERS)]
                    for jg in range(groups)
                ]
                row = (QUARTERS * step + q) * 2 * n_energy + n_energy + height * ROWS
                row = pl.multiple_of(row, ROWS)
                for mode in range(modes):
                    for kg in range(groups):
                        mixed[mode, kg, pl.ds(row, ROWS), :] = total_of(
                            [
                                turned[jg][turn] * coef[mode, kg, jg, turn]
                                for jg in range(groups)
                                for turn in range(QUARTERS)
                            ]
                        )
        return carry

    lax.fori_loop(0, STEPS, mix_step, 0)

    for mode in range(modes):
        shift = shift_ref[mode]
        upper_coef = occupation_ref[mode] + 1.0 - kind
        lower_coef = occupation_ref[mode] + kind
        for kg in range(groups):
            for height in range(heights):

                def right_step(row, carry):
                    values = []
                    for col in range(ORB):
                        first = (row * ORB + col) * 2 * n_energy + n_energy + height * ROWS
                        upper = mixed[mode, kg, pl.ds(first + shift, ROWS), :]
                        lower = mixed[mode, kg, pl.ds(first - shift, ROWS), :]
                        values.append(upper_coef * upper + lower_coef * lower)
                    for n in range(ORB):
                        right_done[mode, kg, height, row * ORB + n] = total_of(
                            [
                                values[col] * coupling[mode * PAIRS + n * ORB + col]
                                for col in range(ORB)
                            ]
                        )
                    return carry

                lax.fori_loop(0, ORB, right_step, 0)

    for kg in range(groups):
        for height in range(heights):

            def left_step(n, carry):
                values = [
                    [right_done[mode, kg, height, row * ORB + n] for row in range(ORB)]
                    for mode in range(modes)
                ]
                for i in range(ORB):
                    both_done[kg, height, i * ORB + n] = total_of(
                        [
                            values[mode][row] * coupling[mode * PAIRS + i * ORB + row]
                            for mode in range(modes)
                            for row in range(ORB)
                        ]
                    )
                return carry

            lax.fori_loop(0, ORB, left_step, 0)

    def unmix_step(step, carry):
        for kg in range(groups):
            for height in range(heights):
                values = [both_done[kg, height, QUARTERS * step + q] for q in range(QUARTERS)]
                for kl, value in enumerate(swap_groups(values, lane, LANES // QUARTERS)):
                    row = ((kg * QUARTERS + kl) * n_energy + height * ROWS) * SLOT + step
                    back[pl.ds(row, ROWS, stride=SLOT), :] = value
        return carry

    lax.fori_loop(0, STEPS, unmix_step, 0)

    home = (back, returned, send_back_sem, recv_back_sem)
    own = exchange_start(*home)
    sends_wait(*there)
    exchange_wait(*home, own)

    def unpack(tile, carry):
        for chunk in range(CHUNKS):
            values = []
            for g in range(PIECES):
                row = slot_of_rank(tile * PIECES + g) + chunk * ROWS
                values.append(returned[pl.ds(pl.multiple_of(row, ROWS), ROWS), :])
            kept = min(ROWS, STEPS - chunk * ROWS)
            for p, value in enumerate(swap_groups(values, lane, GROUP)):
                first = piece_rows(p) + QUARTERS * ROWS * chunk
                if kept == ROWS:
                    outside[tile, pl.ds(first, ROWS, stride=QUARTERS), :] = value
                else:
                    outside[tile, pl.ds(first, kept), :] = value[:kept]
        return carry

    lax.fori_loop(0, tiles, unpack, 0)

    stores = []
    for kind_index in range(2):
        for tile in range(tiles):
            store = pltpu.make_async_copy(
                outside.at[tile, pl.ds(kind_index * 2 * PAIRS, 2 * PAIRS)],
                out_ref.at[kind_index, :, pl.ds(tile * LANES, LANES)],
                local_sem.at[kind_index, tile],
            )
            store.start()
            stores.append(store)
    sends_wait(*home)
    for store in stores:
        store.wait()


def on_device(green_blocks, couple_matrix, occupation, energy_shift, branch_weight, pair_branch):
    n_energy = lax.axis_size("energy")
    n_moment = lax.axis_size("momentum")
    modes = couple_matrix.shape[0]
    width, atoms = green_blocks.shape[3:]
    count = n_energy * n_moment
    tiles = atoms // LANES
    groups = n_moment // QUARTERS
    heights = n_energy // ROWS
    assert green_blocks.shape[1:3] == (1, 1) and width == 2 * PAIRS
    assert couple_matrix.shape[2] == GROUP and STEPS % ROWS == 1
    slots = pltpu.VMEM((count * SLOT, LANES), jnp.float32)
    smem = pl.BlockSpec(memory_space=pltpu.SMEM)
    spare = QUARTERS * (SLOT - STEPS) + QUARTERS
    result = pl.pallas_call(
        functools.partial(kernel, n_energy, n_moment, modes),
        out_shape=jax.ShapeDtypeStruct((2, width, atoms), jnp.float32),
        in_specs=[
            smem,
            smem,
            smem,
            smem,
            pl.BlockSpec(memory_space=pltpu.VMEM),
            pl.BlockSpec(memory_space=pl.ANY),
        ],
        out_specs=pl.BlockSpec(memory_space=pl.ANY),
        scratch_shapes=[
            pltpu.VMEM((tiles, 2 * width + spare, LANES), jnp.float32),
            slots,
            slots,
            pltpu.VMEM((modes, groups, (2 * PAIRS + 1) * n_energy, LANES), jnp.float32),
            pltpu.VMEM((modes * PAIRS, ROWS, LANES), jnp.float32),
            pltpu.VMEM((modes, groups, groups, QUARTERS, ROWS, LANES), jnp.float32),
            pltpu.VMEM((modes, groups, heights, PAIRS, ROWS, LANES), jnp.float32),
            pltpu.VMEM((groups, heights, PAIRS, ROWS, LANES), jnp.float32),
            slots,
            slots,
            pltpu.VMEM((tiles, 2 * width, LANES), jnp.float32),
            pltpu.SemaphoreType.DMA((2, tiles)),
            pltpu.SemaphoreType.DMA((count,)),
            pltpu.SemaphoreType.DMA((count,)),
            pltpu.SemaphoreType.DMA((count,)),
            pltpu.SemaphoreType.DMA((count,)),
        ],
        compiler_params=pltpu.CompilerParams(
            collective_id=0, has_side_effects=True, vmem_limit_bytes=48 * 1024 * 1024
        ),
        name="self_energy",
    )(
        energy_shift,
        occupation,
        branch_weight,
        pair_branch,
        couple_matrix,
        green_blocks.reshape(2, width, atoms),
    )
    return result.reshape(green_blocks.shape)


def solution(mesh):
    in_specs = (
        P(None, "energy", "momentum", None, None),
        P(None, None, ("energy", "momentum")),
        P(),
        P(),
        P(),
        P(),
    )
    out_specs = P(None, "energy", "momentum", None, None)
    return jax.shard_map(
        on_device, mesh=mesh, in_specs=in_specs, out_specs=out_specs, check_vma=False
    )
```

```python
import functools

import jax
import jax.numpy as jnp
from jax import lax
from jax.experimental import pallas as pl
from jax.experimental.pallas import tpu as pltpu
from jax.sharding import PartitionSpec as P

ORB = 10
PAIRS = ORB * ORB
LANES = 128
ROWS = 8
GROUP = 8
PIECES = LANES // GROUP
QUARTERS = 4
STEPS = PAIRS // QUARTERS
SLOT = 32
CHUNKS = SLOT // ROWS
UNROLL = 5
MESH = pl.DeviceIdType.MESH


def swap_groups(arrays, lane, width):
    arrays = list(arrays)
    bit = 1
    while bit < len(arrays):
        low = ((lane // width) & bit) == 0
        for p in range(len(arrays)):
            if p & bit:
                continue
            a, b = arrays[p], arrays[p | bit]
            arrays[p] = jnp.where(low, a, pltpu.roll(b, bit * width, 1))
            arrays[p | bit] = jnp.where(low, pltpu.roll(a, LANES - bit * width, 1), b)
        bit *= 2
    return arrays


def total_of(terms):
    while len(terms) > 1:
        paired = [terms[i] + terms[i + 1] for i in range(0, len(terms) - 1, 2)]
        terms = paired + ([terms[-1]] if len(terms) % 2 else [])
    return terms[0]


def piece_rows(piece):
    quarter, kind, part = piece // 4, (piece // 2) % 2, piece % 2
    return kind * 2 * PAIRS + part * PAIRS + quarter


def kernel(
    n_energy,
    n_moment,
    modes,
    shift_hbm,
    occupation_hbm,
    weight_hbm,
    branch_hbm,
    couple_hbm,
    green_ref,
    out_ref,
    shift_ref,
    occupation_ref,
    weight_ref,
    branch_ref,
    couple_ref,
    inside,
    packed,
    arrived,
    mixed,
    coupling,
    coef,
    right_done,
    both_done,
    back,
    returned,
    outside,
    local_sem,
    small_sem,
    send_sem,
    recv_sem,
    send_back_sem,
    recv_back_sem,
):
    count = n_energy * n_moment
    tiles = green_ref.shape[2] // LANES
    groups = n_moment // QUARTERS
    heights = n_energy // ROWS
    my_energy = lax.axis_index("energy")
    my_moment = lax.axis_index("momentum")

    def slot_of(energy, moment):
        return pl.multiple_of((moment * n_energy + energy) * SLOT, SLOT)

    def slot_of_rank(rank):
        return slot_of(rank // n_moment, rank % n_moment)

    def partner(offset, sign):
        energy = lax.rem(my_energy + sign * (offset // n_moment) + n_energy, n_energy)
        moment = lax.rem(my_moment + sign * (offset % n_moment) + n_moment, n_moment)
        return energy, moment

    loads = []
    for kind in range(2):
        for tile in range(tiles):
            load = pltpu.make_async_copy(
                green_ref.at[kind, :, pl.ds(tile * LANES, LANES)],
                inside.at[tile, pl.ds(kind * 2 * PAIRS, 2 * PAIRS)],
                local_sem.at[kind, tile],
            )
            load.start()
            loads.append(load)

    small_loads = []
    for index, (source, target) in enumerate(
        (
            (couple_hbm, couple_ref),
            (shift_hbm, shift_ref),
            (occupation_hbm, occupation_ref),
            (weight_hbm, weight_ref),
            (branch_hbm, branch_ref),
        )
    ):
        load = pltpu.make_async_copy(source, target, small_sem.at[index])
        load.start()
        small_loads.append(load)

    barrier = pltpu.get_barrier_semaphore()

    def greet(offset, carry):
        energy, moment = partner(offset, 1)
        pl.semaphore_signal(
            barrier, inc=1, device_id={"energy": energy, "momentum": moment}, device_id_type=MESH
        )
        return carry

    lax.fori_loop(1, count, greet, 0)

    lane = lax.broadcasted_iota(jnp.int32, (ROWS, LANES), 1)

    for load in loads:
        load.wait()

    def pack(tile, carry):
        for chunk in range(CHUNKS):
            pieces = [
                inside[
                    tile,
                    pl.ds(piece_rows(p) + QUARTERS * ROWS * chunk, ROWS, stride=QUARTERS),
                    :,
                ]
                for p in range(PIECES)
            ]
            for g, value in enumerate(swap_groups(pieces, lane, GROUP)):
                row = slot_of_rank(tile * PIECES + g) + chunk * ROWS
                packed[pl.ds(pl.multiple_of(row, ROWS), ROWS), :] = value
        return carry

    lax.fori_loop(0, tiles, pack, 0)

    pl.semaphore_wait(barrier, count - 1)

    mine = slot_of(my_energy, my_moment)

    def outgoing(source, target, sends, receives, offset):
        energy, moment = partner(offset, 1)
        return pltpu.make_async_remote_copy(
            src_ref=source.at[pl.ds(slot_of(energy, moment), STEPS)],
            dst_ref=target.at[pl.ds(mine, STEPS)],
            send_sem=sends.at[offset],
            recv_sem=receives.at[offset],
            device_id={"energy": energy, "momentum": moment},
            device_id_type=MESH,
        )

    def incoming(source, target, sends, receives, offset):
        energy, moment = partner(offset, -1)
        return pltpu.make_async_remote_copy(
            src_ref=source.at[pl.ds(mine, STEPS)],
            dst_ref=target.at[pl.ds(slot_of(energy, moment), STEPS)],
            send_sem=sends.at[offset],
            recv_sem=receives.at[offset],
            device_id={"energy": energy, "momentum": moment},
            device_id_type=MESH,
        )

    def exchange_start(source, target, sends, receives):
        def step(offset, carry):
            outgoing(source, target, sends, receives, offset).start()
            return carry

        lax.fori_loop(1, count, step, 0)
        own = pltpu.make_async_copy(
            source.at[pl.ds(mine, STEPS)], target.at[pl.ds(mine, STEPS)], receives.at[0]
        )
        own.start()
        return own

    def exchange_wait(source, target, sends, receives, own):
        def step(offset, carry):
            incoming(source, target, sends, receives, offset).wait_recv()
            return carry

        own.wait()
        lax.fori_loop(1, count, step, 0)

    def sends_wait(source, target, sends, receives):
        def step(offset, carry):
            outgoing(source, target, sends, receives, offset).wait_send()
            return carry

        lax.fori_loop(1, count, step, 0)

    there = (packed, arrived, send_sem, recv_sem)
    own = exchange_start(*there)

    for load in small_loads:
        load.wait()
    spread = (
        lax.broadcasted_iota(jnp.int32, (GROUP, LANES), 1) % GROUP
        == lax.broadcasted_iota(jnp.int32, (GROUP, LANES), 0)
    ).astype(jnp.float32)
    for mode in range(modes):
        wide = lax.dot_general(
            couple_ref[mode],
            spread,
            (((0,), (0,)), ((), ())),
            precision=lax.Precision.HIGHEST,
            preferred_element_type=jnp.float32,
        )
        coupling[pl.ds(mode * PAIRS, PAIRS)] = jnp.broadcast_to(
            wide[:, None, :], (PAIRS, ROWS, LANES)
        )

    lane_moment = lane // (LANES // QUARTERS)
    for mode in range(modes):
        for kg in range(groups):
            for jg in range(groups):
                for turn in range(QUARTERS):
                    value = jnp.zeros((ROWS, LANES), jnp.float32)
                    for kl in range(QUARTERS):
                        k = kg * QUARTERS + kl
                        j = jg * QUARTERS + (kl - turn) % QUARTERS
                        weight = weight_ref[branch_ref[k, j], mode] / n_moment
                        value = jnp.where(lane_moment == kl, weight, value)
                    coef[mode, kg, jg, turn] = value
    kind = ((lane // (2 * GROUP)) % 2).astype(jnp.float32)

    empty = jnp.zeros((n_energy, LANES), jnp.float32)
    for mode in range(modes):
        for kg in range(groups):

            def clear(pair, carry):
                row = pl.multiple_of(pair * 2 * n_energy, ROWS)
                mixed[mode, kg, pl.ds(row, n_energy), :] = empty
                return carry

            lax.fori_loop(0, PAIRS + 1, clear, 0, unroll=True)

    exchange_wait(*there, own)

    def mix_step(step, carry):
        for height in range(heights):
            quarters = []
            for jg in range(groups):
                values = [
                    arrived[
                        pl.ds(
                            ((jg * QUARTERS + jl) * n_energy + height * ROWS) * SLOT + step,
                            ROWS,
                            stride=SLOT,
                        ),
                        :,
                    ]
                    for jl in range(QUARTERS)
                ]
                quarters.append(swap_groups(values, lane, LANES // QUARTERS))
            for q in range(QUARTERS):
                turned = [
                    [quarters[jg][q]]
                    + [pltpu.roll(quarters[jg][q], turn * GROUP * 4, 1) for turn in range(1, QUARTERS)]
                    for jg in range(groups)
                ]
                row = (QUARTERS * step + q) * 2 * n_energy + n_energy + height * ROWS
                row = pl.multiple_of(row, ROWS)
                for mode in range(modes):
                    for kg in range(groups):
                        mixed[mode, kg, pl.ds(row, ROWS), :] = total_of(
                            [
                                turned[jg][turn] * coef[mode, kg, jg, turn]
                                for jg in range(groups)
                                for turn in range(QUARTERS)
                            ]
                        )
        return carry

    lax.fori_loop(0, STEPS, mix_step, 0, unroll=UNROLL)

    for mode in range(modes):
        shift = shift_ref[mode]
        upper_coef = occupation_ref[mode] + 1.0 - kind
        lower_coef = occupation_ref[mode] + kind
        for kg in range(groups):
            for height in range(heights):

                def right_step(row, carry):
                    values = []
                    for col in range(ORB):
                        first = (row * ORB + col) * 2 * n_energy + n_energy + height * ROWS
                        upper = mixed[mode, kg, pl.ds(first + shift, ROWS), :]
                        lower = mixed[mode, kg, pl.ds(first - shift, ROWS), :]
                        values.append(upper_coef * upper + lower_coef * lower)
                    for n in range(ORB):
                        right_done[mode, kg, height, row * ORB + n] = total_of(
                            [
                                values[col] * coupling[mode * PAIRS + n * ORB + col]
                                for col in range(ORB)
                            ]
                        )
                    return carry

                lax.fori_loop(0, ORB, right_step, 0, unroll=2)

    for kg in range(groups):
        for height in range(heights):

            def left_step(n, carry):
                values = [
                    [right_done[mode, kg, height, row * ORB + n] for row in range(ORB)]
                    for mode in range(modes)
                ]
                for i in range(ORB):
                    both_done[kg, height, i * ORB + n] = total_of(
                        [
                            values[mode][row] * coupling[mode * PAIRS + i * ORB + row]
                            for mode in range(modes)
                            for row in range(ORB)
                        ]
                    )
                return carry

            lax.fori_loop(0, ORB, left_step, 0)

    def unmix_step(step, carry):
        for kg in range(groups):
            for height in range(heights):
                values = [both_done[kg, height, QUARTERS * step + q] for q in range(QUARTERS)]
                for kl, value in enumerate(swap_groups(values, lane, LANES // QUARTERS)):
                    row = ((kg * QUARTERS + kl) * n_energy + height * ROWS) * SLOT + step
                    back[pl.ds(row, ROWS, stride=SLOT), :] = value
        return carry

    lax.fori_loop(0, STEPS, unmix_step, 0, unroll=UNROLL)

    home = (back, returned, send_back_sem, recv_back_sem)
    own = exchange_start(*home)
    sends_wait(*there)
    exchange_wait(*home, own)

    def unpack(tile, carry):
        for chunk in range(CHUNKS):
            values = []
            for g in range(PIECES):
                row = slot_of_rank(tile * PIECES + g) + chunk * ROWS
                values.append(returned[pl.ds(pl.multiple_of(row, ROWS), ROWS), :])
            kept = min(ROWS, STEPS - chunk * ROWS)
            for p, value in enumerate(swap_groups(values, lane, GROUP)):
                first = piece_rows(p) + QUARTERS * ROWS * chunk
                if kept == ROWS:
                    outside[tile, pl.ds(first, ROWS, stride=QUARTERS), :] = value
                else:
                    outside[tile, pl.ds(first, kept), :] = value[:kept]
        return carry

    lax.fori_loop(0, tiles, unpack, 0)

    stores = []
    for kind_index in range(2):
        for tile in range(tiles):
            store = pltpu.make_async_copy(
                outside.at[tile, pl.ds(kind_index * 2 * PAIRS, 2 * PAIRS)],
                out_ref.at[kind_index, :, pl.ds(tile * LANES, LANES)],
                local_sem.at[kind_index, tile],
            )
            store.start()
            stores.append(store)
    sends_wait(*home)
    for store in stores:
        store.wait()


def on_device(green_blocks, couple_matrix, occupation, energy_shift, branch_weight, pair_branch):
    n_energy = lax.axis_size("energy")
    n_moment = lax.axis_size("momentum")
    modes = couple_matrix.shape[0]
    width, atoms = green_blocks.shape[3:]
    count = n_energy * n_moment
    tiles = atoms // LANES
    groups = n_moment // QUARTERS
    heights = n_energy // ROWS
    assert green_blocks.shape[1:3] == (1, 1) and width == 2 * PAIRS
    assert couple_matrix.shape[2] == GROUP and STEPS % ROWS == 1
    slots = pltpu.VMEM((count * SLOT, LANES), jnp.float32)
    spare = QUARTERS * (SLOT - STEPS) + QUARTERS
    result = pl.pallas_call(
        functools.partial(kernel, n_energy, n_moment, modes),
        out_shape=jax.ShapeDtypeStruct((2, width, atoms), jnp.float32),
        in_specs=[pl.BlockSpec(memory_space=pl.ANY)] * 6,
        out_specs=pl.BlockSpec(memory_space=pl.ANY),
        scratch_shapes=[
            pltpu.SMEM(energy_shift.shape, jnp.int32),
            pltpu.SMEM(occupation.shape, jnp.float32),
            pltpu.SMEM(branch_weight.shape, jnp.float32),
            pltpu.SMEM(pair_branch.shape, jnp.int32),
            pltpu.VMEM((modes, GROUP, PAIRS), jnp.float32),
            pltpu.VMEM((tiles, 2 * width + spare, LANES), jnp.float32),
            slots,
            slots,
            pltpu.VMEM((modes, groups, (2 * PAIRS + 1) * n_energy, LANES), jnp.float32),
            pltpu.VMEM((modes * PAIRS, ROWS, LANES), jnp.float32),
            pltpu.VMEM((modes, groups, groups, QUARTERS, ROWS, LANES), jnp.float32),
            pltpu.VMEM((modes, groups, heights, PAIRS, ROWS, LANES), jnp.float32),
            pltpu.VMEM((groups, heights, PAIRS, ROWS, LANES), jnp.float32),
            slots,
            slots,
            pltpu.VMEM((tiles, 2 * width, LANES), jnp.float32),
            pltpu.SemaphoreType.DMA((2, tiles)),
            pltpu.SemaphoreType.DMA((5,)),
            pltpu.SemaphoreType.DMA((count,)),
            pltpu.SemaphoreType.DMA((count,)),
            pltpu.SemaphoreType.DMA((count,)),
            pltpu.SemaphoreType.DMA((count,)),
        ],
        compiler_params=pltpu.CompilerParams(
            collective_id=0, has_side_effects=True, vmem_limit_bytes=60 * 1024 * 1024
        ),
        name="self_energy",
    )(
        energy_shift,
        occupation,
        branch_weight,
        pair_branch,
        couple_matrix.transpose(0, 2, 1),
        green_blocks.reshape(2, width, atoms),
    )
    return result.reshape(green_blocks.shape)


def solution(mesh):
    in_specs = (
        P(None, "energy", "momentum", None, None),
        P(None, None, ("energy", "momentum")),
        P(),
        P(),
        P(),
        P(),
    )
    out_specs = P(None, "energy", "momentum", None, None)
    return jax.shard_map(
        on_device, mesh=mesh, in_specs=in_specs, out_specs=out_specs, check_vma=False
    )
```

```python
import functools

import jax
import jax.numpy as jnp
from jax import lax
from jax.experimental import pallas as pl
from jax.experimental.pallas import tpu as pltpu
from jax.sharding import PartitionSpec as P

ORB = 10
PAIRS = ORB * ORB
LANES = 128
ROWS = 8
GROUP = 8
PIECES = LANES // GROUP
QUARTERS = 4
STEPS = PAIRS // QUARTERS
SLOT = 16
THERE = ((0, 15), (15, 10))
HOME = ((0, 10), (10, 15))
UNROLL = 5
MESH = pl.DeviceIdType.MESH


def swap_groups(arrays, lane, width):
    arrays = list(arrays)
    bit = 1
    while bit < len(arrays):
        low = ((lane // width) & bit) == 0
        for p in range(len(arrays)):
            if p & bit:
                continue
            a, b = arrays[p], arrays[p | bit]
            arrays[p] = jnp.where(low, a, pltpu.roll(b, bit * width, 1))
            arrays[p | bit] = jnp.where(low, pltpu.roll(a, LANES - bit * width, 1), b)
        bit *= 2
    return arrays


def total_of(terms):
    while len(terms) > 1:
        paired = [terms[i] + terms[i + 1] for i in range(0, len(terms) - 1, 2)]
        terms = paired + ([terms[-1]] if len(terms) % 2 else [])
    return terms[0]


def piece_rows(piece):
    quarter, kind, part = piece // 4, (piece // 2) % 2, piece % 2
    return kind * 2 * PAIRS + part * PAIRS + quarter


def kernel(
    n_energy,
    n_moment,
    modes,
    shift_hbm,
    occupation_hbm,
    weight_hbm,
    branch_hbm,
    couple_hbm,
    green_ref,
    out_ref,
    shift_ref,
    occupation_ref,
    weight_ref,
    branch_ref,
    couple_ref,
    inside,
    packed_refs,
    arrived_refs,
    mixed,
    coupling,
    coef,
    right_done,
    both_done,
    back_refs,
    returned_refs,
    outside,
    local_sem,
    small_sem,
    send_sem,
    recv_sem,
    own_sem,
    send_back_sem,
    recv_back_sem,
    own_back_sem,
):
    count = n_energy * n_moment
    tiles = green_ref.shape[2] // LANES
    groups = n_moment // QUARTERS
    heights = n_energy // ROWS
    order = sorted(range(n_moment), key=lambda step: -min(step, n_moment - step))
    my_energy = lax.axis_index("energy")
    my_moment = lax.axis_index("momentum")

    def slot_of(energy, moment):
        return pl.multiple_of((moment * n_energy + energy) * SLOT, SLOT)

    def slot_of_rank(rank):
        return slot_of(rank // n_moment, rank % n_moment)

    def for_partners(action):
        def ring(turn, carry):
            energy = lax.rem(my_energy + turn, n_energy)
            for step in order:
                action(energy, lax.rem(my_moment + step, n_moment))
            return carry

        for step in order:
            if step > 0:
                action(my_energy, lax.rem(my_moment + step, n_moment))
        lax.fori_loop(1, n_energy, ring, 0)

    loads = []
    for kind in range(2):
        for tile in range(tiles):
            load = pltpu.make_async_copy(
                green_ref.at[kind, :, pl.ds(tile * LANES, LANES)],
                inside.at[tile, pl.ds(kind * 2 * PAIRS, 2 * PAIRS)],
                local_sem.at[kind, tile],
            )
            load.start()
            loads.append(load)

    small_loads = []
    for index, (source, target) in enumerate(
        (
            (couple_hbm, couple_ref),
            (shift_hbm, shift_ref),
            (occupation_hbm, occupation_ref),
            (weight_hbm, weight_ref),
            (branch_hbm, branch_ref),
        )
    ):
        load = pltpu.make_async_copy(source, target, small_sem.at[index])
        load.start()
        small_loads.append(load)

    barrier = pltpu.get_barrier_semaphore()

    def greet(energy, moment):
        pl.semaphore_signal(
            barrier, inc=1, device_id={"energy": energy, "momentum": moment}, device_id_type=MESH
        )

    for_partners(greet)

    lane = lax.broadcasted_iota(jnp.int32, (ROWS, LANES), 1)

    for load in loads:
        load.wait()

    mine = slot_of(my_energy, my_moment)

    def pack(part):
        begin, rows = THERE[part]

        def pack_tile(tile, carry):
            for place in range(0, rows, ROWS):
                pieces = [
                    inside[
                        tile,
                        pl.ds(piece_rows(p) + QUARTERS * (begin + place), ROWS, stride=QUARTERS),
                        :,
                    ]
                    for p in range(PIECES)
                ]
                for g, value in enumerate(swap_groups(pieces, lane, GROUP)):
                    row = slot_of_rank(tile * PIECES + g) + place
                    packed_refs[part][pl.ds(pl.multiple_of(row, ROWS), ROWS), :] = value
            return carry

        lax.fori_loop(0, tiles, pack_tile, 0)

    def exchange_start(source, target, rows, send, receive, own_sem):
        def start(energy, moment):
            pltpu.make_async_remote_copy(
                src_ref=source.at[pl.ds(slot_of(energy, moment), rows)],
                dst_ref=target.at[pl.ds(mine, rows)],
                send_sem=send,
                recv_sem=receive,
                device_id={"energy": energy, "momentum": moment},
                device_id_type=MESH,
            ).start()

        for_partners(start)
        own = pltpu.make_async_copy(
            source.at[pl.ds(mine, rows)], target.at[pl.ds(mine, rows)], own_sem
        )
        own.start()
        return own

    def wait_all(buffer, rows, semaphore):
        every = buffer.at[pl.ds(0, (count - 1) * rows)]
        pltpu.make_async_copy(every, every, semaphore).wait()

    def start_there(part):
        return exchange_start(
            packed_refs[part],
            arrived_refs[part],
            THERE[part][1],
            send_sem.at[part],
            recv_sem.at[part],
            own_sem.at[part],
        )

    def start_home(part):
        return exchange_start(
            back_refs[part],
            returned_refs[part],
            HOME[part][1],
            send_back_sem.at[part],
            recv_back_sem.at[part],
            own_back_sem.at[part],
        )

    own_there = []
    for part in range(len(THERE)):
        pack(part)
        if part == 0:
            pl.semaphore_wait(barrier, count - 1)
        own_there.append(start_there(part))

    for load in small_loads:
        load.wait()
    spread = (
        lax.broadcasted_iota(jnp.int32, (GROUP, LANES), 1) % GROUP
        == lax.broadcasted_iota(jnp.int32, (GROUP, LANES), 0)
    ).astype(jnp.float32)
    for mode in range(modes):
        wide = lax.dot_general(
            couple_ref[mode],
            spread,
            (((0,), (0,)), ((), ())),
            precision=lax.Precision.HIGHEST,
            preferred_element_type=jnp.float32,
        )
        coupling[pl.ds(mode * PAIRS, PAIRS)] = jnp.broadcast_to(
            wide[:, None, :], (PAIRS, ROWS, LANES)
        )

    lane_moment = lane // (LANES // QUARTERS)
    for mode in range(modes):
        for kg in range(groups):
            for jg in range(groups):
                for turn in range(QUARTERS):
                    value = jnp.zeros((ROWS, LANES), jnp.float32)
                    for kl in range(QUARTERS):
                        k = kg * QUARTERS + kl
                        j = jg * QUARTERS + (kl - turn) % QUARTERS
                        weight = weight_ref[branch_ref[k, j], mode] / n_moment
                        value = jnp.where(lane_moment == kl, weight, value)
                    coef[mode, kg, jg, turn] = value
    kind = ((lane // (2 * GROUP)) % 2).astype(jnp.float32)

    empty = jnp.zeros((n_energy, LANES), jnp.float32)
    for mode in range(modes):
        for kg in range(groups):

            def clear(pair, carry):
                row = pl.multiple_of(pair * 2 * n_energy, ROWS)
                mixed[mode, kg, pl.ds(row, n_energy), :] = empty
                return carry

            lax.fori_loop(0, PAIRS + 1, clear, 0, unroll=True)

    def mix(part):
        begin, rows = THERE[part]
        arrived = arrived_refs[part]

        def mix_step(step, carry):
            for height in range(heights):
                quarters = []
                for jg in range(groups):
                    values = [
                        arrived[
                            pl.ds(
                                ((jg * QUARTERS + jl) * n_energy + height * ROWS) * SLOT + step,
                                ROWS,
                                stride=SLOT,
                            ),
                            :,
                        ]
                        for jl in range(QUARTERS)
                    ]
                    quarters.append(swap_groups(values, lane, LANES // QUARTERS))
                for q in range(QUARTERS):
                    turned = [
                        [quarters[jg][q]]
                        + [
                            pltpu.roll(quarters[jg][q], turn * (LANES // QUARTERS), 1)
                            for turn in range(1, QUARTERS)
                        ]
                        for jg in range(groups)
                    ]
                    pair = QUARTERS * (begin + step) + q
                    row = pl.multiple_of((pair * 2 + 1) * n_energy + height * ROWS, ROWS)
                    for mode in range(modes):
                        for kg in range(groups):
                            mixed[mode, kg, pl.ds(row, ROWS), :] = total_of(
                                [
                                    turned[jg][turn] * coef[mode, kg, jg, turn]
                                    for jg in range(groups)
                                    for turn in range(QUARTERS)
                                ]
                            )
            return carry

        lax.fori_loop(0, rows, mix_step, 0, unroll=UNROLL)

    def multiply_right(part):
        begin, rows = THERE[part]
        for mode in range(modes):
            shift = shift_ref[mode]
            upper_coef = occupation_ref[mode] + 1.0 - kind
            lower_coef = occupation_ref[mode] + kind
            for kg in range(groups):
                for height in range(heights):

                    def right_step(row, carry):
                        values = []
                        for col in range(ORB):
                            first = ((row * ORB + col) * 2 + 1) * n_energy + height * ROWS
                            upper = mixed[mode, kg, pl.ds(first + shift, ROWS), :]
                            lower = mixed[mode, kg, pl.ds(first - shift, ROWS), :]
                            values.append(upper_coef * upper + lower_coef * lower)
                        for n in range(ORB):
                            right_done[mode, kg, height, row * ORB + n] = total_of(
                                [
                                    values[col] * coupling[mode * PAIRS + n * ORB + col]
                                    for col in range(ORB)
                                ]
                            )
                        return carry

                    lax.fori_loop(
                        begin * QUARTERS // ORB,
                        (begin + rows) * QUARTERS // ORB,
                        right_step,
                        0,
                        unroll=2,
                    )

    def multiply_left(part):
        begin, rows = HOME[part]
        back = back_refs[part]
        for kg in range(groups):
            for height in range(heights):

                def left_step(n, carry):
                    values = [
                        [right_done[mode, kg, height, row * ORB + n] for row in range(ORB)]
                        for mode in range(modes)
                    ]
                    for i in range(begin * QUARTERS // ORB, (begin + rows) * QUARTERS // ORB):
                        both_done[kg, height, i * ORB + n] = total_of(
                            [
                                values[mode][row] * coupling[mode * PAIRS + i * ORB + row]
                                for mode in range(modes)
                                for row in range(ORB)
                            ]
                        )
                    return carry

                lax.fori_loop(0, ORB, left_step, 0)

        def unmix_step(step, carry):
            for kg in range(groups):
                for height in range(heights):
                    pair = QUARTERS * (begin + step)
                    values = [both_done[kg, height, pair + q] for q in range(QUARTERS)]
                    for kl, value in enumerate(swap_groups(values, lane, LANES // QUARTERS)):
                        row = ((kg * QUARTERS + kl) * n_energy + height * ROWS) * SLOT + step
                        back[pl.ds(row, ROWS, stride=SLOT), :] = value
            return carry

        lax.fori_loop(0, rows, unmix_step, 0, unroll=UNROLL)

    for part, (_, rows) in enumerate(THERE):
        own_there[part].wait()
        wait_all(arrived_refs[part], rows, recv_sem.at[part])
        mix(part)
        multiply_right(part)
    own_home = []
    for part in range(len(HOME)):
        multiply_left(part)
        own_home.append(start_home(part))
    for part, (_, rows) in enumerate(THERE):
        wait_all(packed_refs[part], rows, send_sem.at[part])

    for part, (begin, rows) in enumerate(HOME):
        own_home[part].wait()
        wait_all(returned_refs[part], rows, recv_back_sem.at[part])

        def unpack(tile, carry):
            for place in range(0, rows, ROWS):
                values = []
                for g in range(PIECES):
                    row = slot_of_rank(tile * PIECES + g) + place
                    values.append(
                        returned_refs[part][pl.ds(pl.multiple_of(row, ROWS), ROWS), :]
                    )
                kept = min(ROWS, rows - place)
                for p, value in enumerate(swap_groups(values, lane, GROUP)):
                    first = piece_rows(p) + QUARTERS * (begin + place)
                    outside[tile, pl.ds(first, kept, stride=QUARTERS), :] = value[:kept]
            return carry

        lax.fori_loop(0, tiles, unpack, 0)

    stores = []
    for kind_index in range(2):
        for tile in range(tiles):
            store = pltpu.make_async_copy(
                outside.at[tile, pl.ds(kind_index * 2 * PAIRS, 2 * PAIRS)],
                out_ref.at[kind_index, :, pl.ds(tile * LANES, LANES)],
                local_sem.at[kind_index, tile],
            )
            store.start()
            stores.append(store)
    for part, (_, rows) in enumerate(HOME):
        wait_all(back_refs[part], rows, send_back_sem.at[part])
    for store in stores:
        store.wait()


def on_device(green_blocks, couple_matrix, occupation, energy_shift, branch_weight, pair_branch):
    n_energy = lax.axis_size("energy")
    n_moment = lax.axis_size("momentum")
    modes = couple_matrix.shape[0]
    width, atoms = green_blocks.shape[3:]
    count = n_energy * n_moment
    tiles = atoms // LANES
    groups = n_moment // QUARTERS
    heights = n_energy // ROWS
    assert green_blocks.shape[1:3] == (1, 1) and width == 2 * PAIRS
    assert couple_matrix.shape[2] == GROUP
    slots = pltpu.VMEM((count * SLOT, LANES), jnp.float32)
    there_slots, home_slots = (slots,) * len(THERE), (slots,) * len(HOME)
    there_sems = pltpu.SemaphoreType.DMA((len(THERE),))
    home_sems = pltpu.SemaphoreType.DMA((len(HOME),))
    spare = QUARTERS * ROWS
    result = pl.pallas_call(
        functools.partial(kernel, n_energy, n_moment, modes),
        out_shape=jax.ShapeDtypeStruct((2, width, atoms), jnp.float32),
        in_specs=[pl.BlockSpec(memory_space=pl.ANY)] * 6,
        out_specs=pl.BlockSpec(memory_space=pl.ANY),
        scratch_shapes=[
            pltpu.SMEM(energy_shift.shape, jnp.int32),
            pltpu.SMEM(occupation.shape, jnp.float32),
            pltpu.SMEM(branch_weight.shape, jnp.float32),
            pltpu.SMEM(pair_branch.shape, jnp.int32),
            pltpu.VMEM((modes, GROUP, PAIRS), jnp.float32),
            pltpu.VMEM((tiles, 2 * width + spare, LANES), jnp.float32),
            there_slots,
            there_slots,
            pltpu.VMEM((modes, groups, (2 * PAIRS + 1) * n_energy, LANES), jnp.float32),
            pltpu.VMEM((modes * PAIRS, ROWS, LANES), jnp.float32),
            pltpu.VMEM((modes, groups, groups, QUARTERS, ROWS, LANES), jnp.float32),
            pltpu.VMEM((modes, groups, heights, PAIRS, ROWS, LANES), jnp.float32),
            pltpu.VMEM((groups, heights, PAIRS, ROWS, LANES), jnp.float32),
            home_slots,
            home_slots,
            pltpu.VMEM((tiles, 2 * width, LANES), jnp.float32),
            pltpu.SemaphoreType.DMA((2, tiles)),
            pltpu.SemaphoreType.DMA((5,)),
            there_sems,
            there_sems,
            there_sems,
            home_sems,
            home_sems,
            home_sems,
        ],
        compiler_params=pltpu.CompilerParams(
            collective_id=0, has_side_effects=True, vmem_limit_bytes=60 * 1024 * 1024
        ),
        name="self_energy",
    )(
        energy_shift,
        occupation,
        branch_weight,
        pair_branch,
        couple_matrix.transpose(0, 2, 1),
        green_blocks.reshape(2, width, atoms),
    )
    return result.reshape(green_blocks.shape)


def solution(mesh):
    in_specs = (
        P(None, "energy", "momentum", None, None),
        P(None, None, ("energy", "momentum")),
        P(),
        P(),
        P(),
        P(),
    )
    out_specs = P(None, "energy", "momentum", None, None)
    return jax.shard_map(
        on_device, mesh=mesh, in_specs=in_specs, out_specs=out_specs, check_vma=False
    )
```

```python
import functools

import jax
import jax.numpy as jnp
from jax import lax
from jax.experimental import pallas as pl
from jax.experimental.pallas import tpu as pltpu
from jax.sharding import PartitionSpec as P

ORB = 10
PAIRS = ORB * ORB
LANES = 128
ROWS = 8
GROUP = 8
PIECES = LANES // GROUP
QUARTERS = 4
STEPS = PAIRS // QUARTERS
SLOT = 16
THERE = ((0, 10), (10, 10), (20, 5))
HOME = ((0, 5), (5, 10), (15, 10))
UNROLL = 5
MESH = pl.DeviceIdType.MESH


def swap_groups(arrays, lane, width):
    arrays = list(arrays)
    bit = 1
    while bit < len(arrays):
        low = ((lane // width) & bit) == 0
        for p in range(len(arrays)):
            if p & bit:
                continue
            a, b = arrays[p], arrays[p | bit]
            arrays[p] = jnp.where(low, a, pltpu.roll(b, bit * width, 1))
            arrays[p | bit] = jnp.where(low, pltpu.roll(a, LANES - bit * width, 1), b)
        bit *= 2
    return arrays


def total_of(terms):
    while len(terms) > 1:
        paired = [terms[i] + terms[i + 1] for i in range(0, len(terms) - 1, 2)]
        terms = paired + ([terms[-1]] if len(terms) % 2 else [])
    return terms[0]


def piece_rows(piece):
    quarter, kind, part = piece // 4, (piece // 2) % 2, piece % 2
    return kind * 2 * PAIRS + part * PAIRS + quarter


def kernel(
    n_energy,
    n_moment,
    modes,
    shift_hbm,
    occupation_hbm,
    weight_hbm,
    branch_hbm,
    couple_hbm,
    green_ref,
    out_ref,
    shift_ref,
    occupation_ref,
    weight_ref,
    branch_ref,
    couple_ref,
    inside,
    packed_refs,
    arrived_refs,
    mixed,
    coupling,
    coef,
    right_done,
    both_done,
    back_refs,
    returned_refs,
    outside,
    local_sem,
    small_sem,
    send_sem,
    recv_sem,
    own_sem,
    send_back_sem,
    recv_back_sem,
    own_back_sem,
):
    count = n_energy * n_moment
    tiles = green_ref.shape[2] // LANES
    groups = n_moment // QUARTERS
    heights = n_energy // ROWS
    order = sorted(range(n_moment), key=lambda step: -min(step, n_moment - step))
    my_energy = lax.axis_index("energy")
    my_moment = lax.axis_index("momentum")

    def slot_of(energy, moment):
        return pl.multiple_of((moment * n_energy + energy) * SLOT, SLOT)

    def slot_of_rank(rank):
        return slot_of(rank // n_moment, rank % n_moment)

    def for_partners(action):
        def ring(turn, carry):
            energy = lax.rem(my_energy + turn, n_energy)
            for step in order:
                action(energy, lax.rem(my_moment + step, n_moment))
            return carry

        for step in order:
            if step > 0:
                action(my_energy, lax.rem(my_moment + step, n_moment))
        lax.fori_loop(1, n_energy, ring, 0)

    loads = []
    for kind in range(2):
        for tile in range(tiles):
            load = pltpu.make_async_copy(
                green_ref.at[kind, :, pl.ds(tile * LANES, LANES)],
                inside.at[tile, pl.ds(kind * 2 * PAIRS, 2 * PAIRS)],
                local_sem.at[kind, tile],
            )
            load.start()
            loads.append(load)

    small_loads = []
    for index, (source, target) in enumerate(
        (
            (couple_hbm, couple_ref),
            (shift_hbm, shift_ref),
            (occupation_hbm, occupation_ref),
            (weight_hbm, weight_ref),
            (branch_hbm, branch_ref),
        )
    ):
        load = pltpu.make_async_copy(source, target, small_sem.at[index])
        load.start()
        small_loads.append(load)

    barrier = pltpu.get_barrier_semaphore()

    def greet(energy, moment):
        pl.semaphore_signal(
            barrier, inc=1, device_id={"energy": energy, "momentum": moment}, device_id_type=MESH
        )

    for_partners(greet)

    lane = lax.broadcasted_iota(jnp.int32, (ROWS, LANES), 1)

    for load in loads:
        load.wait()

    mine = slot_of(my_energy, my_moment)

    def pack(part):
        begin, rows = THERE[part]

        def pack_tile(tile, carry):
            for place in range(0, rows, ROWS):
                pieces = [
                    inside[
                        tile,
                        pl.ds(piece_rows(p) + QUARTERS * (begin + place), ROWS, stride=QUARTERS),
                        :,
                    ]
                    for p in range(PIECES)
                ]
                for g, value in enumerate(swap_groups(pieces, lane, GROUP)):
                    row = slot_of_rank(tile * PIECES + g) + place
                    packed_refs[part][pl.ds(pl.multiple_of(row, ROWS), ROWS), :] = value
            return carry

        lax.fori_loop(0, tiles, pack_tile, 0)

    def exchange_start(source, target, rows, send, receive, own_sem):
        def start(energy, moment):
            pltpu.make_async_remote_copy(
                src_ref=source.at[pl.ds(slot_of(energy, moment), rows)],
                dst_ref=target.at[pl.ds(mine, rows)],
                send_sem=send,
                recv_sem=receive,
                device_id={"energy": energy, "momentum": moment},
                device_id_type=MESH,
            ).start()

        for_partners(start)
        own = pltpu.make_async_copy(
            source.at[pl.ds(mine, rows)], target.at[pl.ds(mine, rows)], own_sem
        )
        own.start()
        return own

    def wait_all(buffer, rows, semaphore):
        every = buffer.at[pl.ds(0, (count - 1) * rows)]
        pltpu.make_async_copy(every, every, semaphore).wait()

    def start_there(part):
        return exchange_start(
            packed_refs[part],
            arrived_refs[part],
            THERE[part][1],
            send_sem.at[part],
            recv_sem.at[part],
            own_sem.at[part],
        )

    def start_home(part):
        return exchange_start(
            back_refs[part],
            returned_refs[part],
            HOME[part][1],
            send_back_sem.at[part],
            recv_back_sem.at[part],
            own_back_sem.at[part],
        )

    own_there = []
    for part in range(len(THERE)):
        pack(part)
        if part == 0:
            pl.semaphore_wait(barrier, count - 1)
        own_there.append(start_there(part))

    for load in small_loads:
        load.wait()
    spread = (
        lax.broadcasted_iota(jnp.int32, (GROUP, LANES), 1) % GROUP
        == lax.broadcasted_iota(jnp.int32, (GROUP, LANES), 0)
    ).astype(jnp.float32)
    for mode in range(modes):
        wide = lax.dot_general(
            couple_ref[mode],
            spread,
            (((0,), (0,)), ((), ())),
            precision=lax.Precision.HIGHEST,
            preferred_element_type=jnp.float32,
        )
        coupling[pl.ds(mode * PAIRS, PAIRS)] = jnp.broadcast_to(
            wide[:, None, :], (PAIRS, ROWS, LANES)
        )

    lane_moment = lane // (LANES // QUARTERS)
    for mode in range(modes):
        for kg in range(groups):
            for jg in range(groups):
                for turn in range(QUARTERS):
                    value = jnp.zeros((ROWS, LANES), jnp.float32)
                    for kl in range(QUARTERS):
                        k = kg * QUARTERS + kl
                        j = jg * QUARTERS + (kl - turn) % QUARTERS
                        weight = weight_ref[branch_ref[k, j], mode] / n_moment
                        value = jnp.where(lane_moment == kl, weight, value)
                    coef[mode, kg, jg, turn] = value
    kind = ((lane // (2 * GROUP)) % 2).astype(jnp.float32)

    empty = jnp.zeros((n_energy, LANES), jnp.float32)
    for mode in range(modes):
        for kg in range(groups):

            def clear(pair, carry):
                row = pl.multiple_of(pair * 2 * n_energy, ROWS)
                mixed[mode, kg, pl.ds(row, n_energy), :] = empty
                return carry

            lax.fori_loop(0, PAIRS + 1, clear, 0, unroll=True)

    def mix(part):
        begin, rows = THERE[part]
        arrived = arrived_refs[part]

        def mix_step(step, carry):
            for height in range(heights):
                quarters = []
                for jg in range(groups):
                    values = [
                        arrived[
                            pl.ds(
                                ((jg * QUARTERS + jl) * n_energy + height * ROWS) * SLOT + step,
                                ROWS,
                                stride=SLOT,
                            ),
                            :,
                        ]
                        for jl in range(QUARTERS)
                    ]
                    quarters.append(swap_groups(values, lane, LANES // QUARTERS))
                for q in range(QUARTERS):
                    turned = [
                        [quarters[jg][q]]
                        + [
                            pltpu.roll(quarters[jg][q], turn * (LANES // QUARTERS), 1)
                            for turn in range(1, QUARTERS)
                        ]
                        for jg in range(groups)
                    ]
                    pair = QUARTERS * (begin + step) + q
                    row = pl.multiple_of((pair * 2 + 1) * n_energy + height * ROWS, ROWS)
                    for mode in range(modes):
                        for kg in range(groups):
                            mixed[mode, kg, pl.ds(row, ROWS), :] = total_of(
                                [
                                    turned[jg][turn] * coef[mode, kg, jg, turn]
                                    for jg in range(groups)
                                    for turn in range(QUARTERS)
                                ]
                            )
            return carry

        lax.fori_loop(0, rows, mix_step, 0, unroll=UNROLL)

    def multiply_right(part):
        begin, rows = THERE[part]
        for mode in range(modes):
            shift = shift_ref[mode]
            upper_coef = occupation_ref[mode] + 1.0 - kind
            lower_coef = occupation_ref[mode] + kind
            for kg in range(groups):
                for height in range(heights):

                    def right_step(row, carry):
                        values = []
                        for col in range(ORB):
                            first = ((row * ORB + col) * 2 + 1) * n_energy + height * ROWS
                            upper = mixed[mode, kg, pl.ds(first + shift, ROWS), :]
                            lower = mixed[mode, kg, pl.ds(first - shift, ROWS), :]
                            values.append(upper_coef * upper + lower_coef * lower)
                        for n in range(ORB):
                            right_done[mode, kg, height, row * ORB + n] = total_of(
                                [
                                    values[col] * coupling[mode * PAIRS + n * ORB + col]
                                    for col in range(ORB)
                                ]
                            )
                        return carry

                    lax.fori_loop(
                        begin * QUARTERS // ORB,
                        (begin + rows) * QUARTERS // ORB,
                        right_step,
                        0,
                        unroll=2,
                    )

    def multiply_left(part):
        begin, rows = HOME[part]
        back = back_refs[part]
        for kg in range(groups):
            for height in range(heights):

                def left_step(n, carry):
                    values = [
                        [right_done[mode, kg, height, row * ORB + n] for row in range(ORB)]
                        for mode in range(modes)
                    ]
                    for i in range(begin * QUARTERS // ORB, (begin + rows) * QUARTERS // ORB):
                        both_done[kg, height, i * ORB + n] = total_of(
                            [
                                values[mode][row] * coupling[mode * PAIRS + i * ORB + row]
                                for mode in range(modes)
                                for row in range(ORB)
                            ]
                        )
                    return carry

                lax.fori_loop(0, ORB, left_step, 0, unroll=2)

        def unmix_step(step, carry):
            for kg in range(groups):
                for height in range(heights):
                    pair = QUARTERS * (begin + step)
                    values = [both_done[kg, height, pair + q] for q in range(QUARTERS)]
                    for kl, value in enumerate(swap_groups(values, lane, LANES // QUARTERS)):
                        row = ((kg * QUARTERS + kl) * n_energy + height * ROWS) * SLOT + step
                        back[pl.ds(row, ROWS, stride=SLOT), :] = value
            return carry

        lax.fori_loop(0, rows, unmix_step, 0, unroll=UNROLL)

    for part, (_, rows) in enumerate(THERE):
        own_there[part].wait()
        wait_all(arrived_refs[part], rows, recv_sem.at[part])
        mix(part)
        multiply_right(part)
    own_home = []
    for part in range(len(HOME)):
        multiply_left(part)
        own_home.append(start_home(part))
    for part, (_, rows) in enumerate(THERE):
        wait_all(packed_refs[part], rows, send_sem.at[part])

    for part, (begin, rows) in enumerate(HOME):
        own_home[part].wait()
        wait_all(returned_refs[part], rows, recv_back_sem.at[part])

        def unpack(tile, carry):
            for place in range(0, rows, ROWS):
                values = []
                for g in range(PIECES):
                    row = slot_of_rank(tile * PIECES + g) + place
                    values.append(
                        returned_refs[part][pl.ds(pl.multiple_of(row, ROWS), ROWS), :]
                    )
                kept = min(ROWS, rows - place)
                for p, value in enumerate(swap_groups(values, lane, GROUP)):
                    first = piece_rows(p) + QUARTERS * (begin + place)
                    outside[tile, pl.ds(first, kept, stride=QUARTERS), :] = value[:kept]
            return carry

        lax.fori_loop(0, tiles, unpack, 0)

    stores = []
    for kind_index in range(2):
        for tile in range(tiles):
            store = pltpu.make_async_copy(
                outside.at[tile, pl.ds(kind_index * 2 * PAIRS, 2 * PAIRS)],
                out_ref.at[kind_index, :, pl.ds(tile * LANES, LANES)],
                local_sem.at[kind_index, tile],
            )
            store.start()
            stores.append(store)
    for part, (_, rows) in enumerate(HOME):
        wait_all(back_refs[part], rows, send_back_sem.at[part])
    for store in stores:
        store.wait()


def on_device(green_blocks, couple_matrix, occupation, energy_shift, branch_weight, pair_branch):
    n_energy = lax.axis_size("energy")
    n_moment = lax.axis_size("momentum")
    modes = couple_matrix.shape[0]
    width, atoms = green_blocks.shape[3:]
    count = n_energy * n_moment
    tiles = atoms // LANES
    groups = n_moment // QUARTERS
    heights = n_energy // ROWS
    assert green_blocks.shape[1:3] == (1, 1) and width == 2 * PAIRS
    assert couple_matrix.shape[2] == GROUP
    slots = pltpu.VMEM((count * SLOT, LANES), jnp.float32)
    there_slots, home_slots = (slots,) * len(THERE), (slots,) * len(HOME)
    there_sems = pltpu.SemaphoreType.DMA((len(THERE),))
    home_sems = pltpu.SemaphoreType.DMA((len(HOME),))
    spare = QUARTERS * ROWS
    result = pl.pallas_call(
        functools.partial(kernel, n_energy, n_moment, modes),
        out_shape=pltpu.VMEM((2, width, atoms), jnp.float32),
        in_specs=[pl.BlockSpec(memory_space=pl.ANY)] * 6,
        out_specs=pl.BlockSpec(memory_space=pl.ANY),
        scratch_shapes=[
            pltpu.SMEM(energy_shift.shape, jnp.int32),
            pltpu.SMEM(occupation.shape, jnp.float32),
            pltpu.SMEM(branch_weight.shape, jnp.float32),
            pltpu.SMEM(pair_branch.shape, jnp.int32),
            pltpu.VMEM((modes, GROUP, PAIRS), jnp.float32),
            pltpu.VMEM((tiles, 2 * width + spare, LANES), jnp.float32),
            there_slots,
            there_slots,
            pltpu.VMEM((modes, groups, (2 * PAIRS + 1) * n_energy, LANES), jnp.float32),
            pltpu.VMEM((modes * PAIRS, ROWS, LANES), jnp.float32),
            pltpu.VMEM((modes, groups, groups, QUARTERS, ROWS, LANES), jnp.float32),
            pltpu.VMEM((modes, groups, heights, PAIRS, ROWS, LANES), jnp.float32),
            pltpu.VMEM((groups, heights, PAIRS, ROWS, LANES), jnp.float32),
            home_slots,
            home_slots,
            pltpu.VMEM((tiles, 2 * width, LANES), jnp.float32),
            pltpu.SemaphoreType.DMA((2, tiles)),
            pltpu.SemaphoreType.DMA((5,)),
            there_sems,
            there_sems,
            there_sems,
            home_sems,
            home_sems,
            home_sems,
        ],
        compiler_params=pltpu.CompilerParams(
            collective_id=0, has_side_effects=True, vmem_limit_bytes=60 * 1024 * 1024
        ),
        name="self_energy",
    )(
        energy_shift,
        occupation,
        branch_weight,
        pair_branch,
        couple_matrix.transpose(0, 2, 1),
        green_blocks.reshape(2, width, atoms),
    )
    return result.reshape(green_blocks.shape)


def solution(mesh):
    in_specs = (
        P(None, "energy", "momentum", None, None),
        P(None, None, ("energy", "momentum")),
        P(),
        P(),
        P(),
        P(),
    )
    out_specs = P(None, "energy", "momentum", None, None)
    return jax.shard_map(
        on_device, mesh=mesh, in_specs=in_specs, out_specs=out_specs, check_vma=False
    )
```

```python
import functools

import jax
import jax.numpy as jnp
from jax import lax
from jax.experimental import pallas as pl
from jax.experimental.pallas import tpu as pltpu
from jax.sharding import PartitionSpec as P

ORB = 10
PAIRS = ORB * ORB
LANES = 128
ROWS = 8
GROUP = 8
PIECES = LANES // GROUP
QUARTERS = 4
STEPS = PAIRS // QUARTERS
SLOT = 16
THERE = ((0, 10), (10, 10), (20, 5))
HOME = ((0, 5), (5, 15), (20, 5))
UNROLL = 5
MESH = pl.DeviceIdType.MESH


def swap_groups(arrays, lane, width):
    arrays = list(arrays)
    bit = 1
    while bit < len(arrays):
        low = ((lane // width) & bit) == 0
        for p in range(len(arrays)):
            if p & bit:
                continue
            a, b = arrays[p], arrays[p | bit]
            arrays[p] = jnp.where(low, a, pltpu.roll(b, bit * width, 1))
            arrays[p | bit] = jnp.where(low, pltpu.roll(a, LANES - bit * width, 1), b)
        bit *= 2
    return arrays


def total_of(terms):
    while len(terms) > 1:
        paired = [terms[i] + terms[i + 1] for i in range(0, len(terms) - 1, 2)]
        terms = paired + ([terms[-1]] if len(terms) % 2 else [])
    return terms[0]


def piece_rows(piece):
    quarter, kind, part = piece // 4, (piece // 2) % 2, piece % 2
    return kind * 2 * PAIRS + part * PAIRS + quarter


def kernel(
    n_energy,
    n_moment,
    modes,
    shift_hbm,
    occupation_hbm,
    weight_hbm,
    branch_hbm,
    couple_hbm,
    green_ref,
    out_ref,
    shift_ref,
    occupation_ref,
    weight_ref,
    branch_ref,
    couple_ref,
    inside,
    packed_refs,
    arrived_refs,
    mixed,
    coupling,
    coef,
    right_done,
    both_done,
    back_refs,
    returned_refs,
    outside,
    local_sem,
    small_sem,
    send_sem,
    recv_sem,
    own_sem,
    send_back_sem,
    recv_back_sem,
    own_back_sem,
):
    count = n_energy * n_moment
    tiles = green_ref.shape[2] // LANES
    groups = n_moment // QUARTERS
    heights = n_energy // ROWS
    my_energy = lax.axis_index("energy")
    my_moment = lax.axis_index("momentum")

    def slot_of(energy, moment):
        return pl.multiple_of((moment * n_energy + energy) * SLOT, SLOT)

    def slot_of_rank(rank):
        return slot_of(rank // n_moment, rank % n_moment)

    def across(flip):
        moment, bit = my_moment, 1
        while bit <= flip:
            if flip & bit:
                moment = moment + bit - 2 * bit * ((my_moment // bit) % 2)
            bit *= 2
        return moment

    def for_partners(action):
        for flip in reversed(range(n_moment)):
            moment = across(flip)

            def ring(turn, carry):
                action(lax.rem(my_energy + turn, n_energy), moment)
                return carry

            lax.fori_loop(0 if flip else 1, n_energy, ring, 0, unroll=2)

    loads = []
    for kind in range(2):
        for tile in range(tiles):
            load = pltpu.make_async_copy(
                green_ref.at[kind, :, pl.ds(tile * LANES, LANES)],
                inside.at[tile, pl.ds(kind * 2 * PAIRS, 2 * PAIRS)],
                local_sem.at[kind, tile],
            )
            load.start()
            loads.append(load)

    small_loads = []
    for index, (source, target) in enumerate(
        (
            (couple_hbm, couple_ref),
            (shift_hbm, shift_ref),
            (occupation_hbm, occupation_ref),
            (weight_hbm, weight_ref),
            (branch_hbm, branch_ref),
        )
    ):
        load = pltpu.make_async_copy(source, target, small_sem.at[index])
        load.start()
        small_loads.append(load)

    barrier = pltpu.get_barrier_semaphore()

    def greet(energy, moment):
        pl.semaphore_signal(
            barrier, inc=1, device_id={"energy": energy, "momentum": moment}, device_id_type=MESH
        )

    for_partners(greet)

    lane = lax.broadcasted_iota(jnp.int32, (ROWS, LANES), 1)

    for load in loads:
        load.wait()

    mine = slot_of(my_energy, my_moment)

    def pack(part):
        begin, rows = THERE[part]

        def pack_tile(tile, carry):
            for place in range(0, rows, ROWS):
                pieces = [
                    inside[
                        tile,
                        pl.ds(piece_rows(p) + QUARTERS * (begin + place), ROWS, stride=QUARTERS),
                        :,
                    ]
                    for p in range(PIECES)
                ]
                for g, value in enumerate(swap_groups(pieces, lane, GROUP)):
                    row = slot_of_rank(tile * PIECES + g) + place
                    packed_refs[part][pl.ds(pl.multiple_of(row, ROWS), ROWS), :] = value
            return carry

        lax.fori_loop(0, tiles, pack_tile, 0)

    def exchange_start(source, target, rows, send, receive, own_sem):
        def start(energy, moment):
            pltpu.make_async_remote_copy(
                src_ref=source.at[pl.ds(slot_of(energy, moment), rows)],
                dst_ref=target.at[pl.ds(mine, rows)],
                send_sem=send,
                recv_sem=receive,
                device_id={"energy": energy, "momentum": moment},
                device_id_type=MESH,
            ).start()

        for_partners(start)
        own = pltpu.make_async_copy(
            source.at[pl.ds(mine, rows)], target.at[pl.ds(mine, rows)], own_sem
        )
        own.start()
        return own

    def wait_all(buffer, rows, semaphore):
        every = buffer.at[pl.ds(0, (count - 1) * rows)]
        pltpu.make_async_copy(every, every, semaphore).wait()

    def start_there(part):
        return exchange_start(
            packed_refs[part],
            arrived_refs[part],
            THERE[part][1],
            send_sem.at[part],
            recv_sem.at[part],
            own_sem.at[part],
        )

    def start_home(part):
        return exchange_start(
            back_refs[part],
            returned_refs[part],
            HOME[part][1],
            send_back_sem.at[part],
            recv_back_sem.at[part],
            own_back_sem.at[part],
        )

    own_there = []
    for part in range(len(THERE)):
        pack(part)
        if part == 0:
            pl.semaphore_wait(barrier, count - 1)
        own_there.append(start_there(part))

    for load in small_loads:
        load.wait()
    spread = (
        lax.broadcasted_iota(jnp.int32, (GROUP, LANES), 1) % GROUP
        == lax.broadcasted_iota(jnp.int32, (GROUP, LANES), 0)
    ).astype(jnp.float32)
    for mode in range(modes):
        wide = lax.dot_general(
            couple_ref[mode],
            spread,
            (((0,), (0,)), ((), ())),
            precision=lax.Precision.HIGHEST,
            preferred_element_type=jnp.float32,
        )
        coupling[pl.ds(mode * PAIRS, PAIRS)] = jnp.broadcast_to(
            wide[:, None, :], (PAIRS, ROWS, LANES)
        )

    lane_moment = lane // (LANES // QUARTERS)
    for mode in range(modes):
        for kg in range(groups):
            for jg in range(groups):
                for turn in range(QUARTERS):
                    value = jnp.zeros((ROWS, LANES), jnp.float32)
                    for kl in range(QUARTERS):
                        k = kg * QUARTERS + kl
                        j = jg * QUARTERS + (kl - turn) % QUARTERS
                        weight = weight_ref[branch_ref[k, j], mode] / n_moment
                        value = jnp.where(lane_moment == kl, weight, value)
                    coef[mode, kg, jg, turn] = value
    kind = ((lane // (2 * GROUP)) % 2).astype(jnp.float32)

    empty = jnp.zeros((n_energy, LANES), jnp.float32)
    for mode in range(modes):
        for kg in range(groups):

            def clear(pair, carry):
                row = pl.multiple_of(pair * 2 * n_energy, ROWS)
                mixed[mode, kg, pl.ds(row, n_energy), :] = empty
                return carry

            lax.fori_loop(0, PAIRS + 1, clear, 0, unroll=True)

    def mix(part):
        begin, rows = THERE[part]
        arrived = arrived_refs[part]

        def mix_step(step, carry):
            for height in range(heights):
                quarters = []
                for jg in range(groups):
                    values = [
                        arrived[
                            pl.ds(
                                ((jg * QUARTERS + jl) * n_energy + height * ROWS) * SLOT + step,
                                ROWS,
                                stride=SLOT,
                            ),
                            :,
                        ]
                        for jl in range(QUARTERS)
                    ]
                    quarters.append(swap_groups(values, lane, LANES // QUARTERS))
                for q in range(QUARTERS):
                    turned = [
                        [quarters[jg][q]]
                        + [
                            pltpu.roll(quarters[jg][q], turn * (LANES // QUARTERS), 1)
                            for turn in range(1, QUARTERS)
                        ]
                        for jg in range(groups)
                    ]
                    pair = QUARTERS * (begin + step) + q
                    row = pl.multiple_of((pair * 2 + 1) * n_energy + height * ROWS, ROWS)
                    for mode in range(modes):
                        for kg in range(groups):
                            mixed[mode, kg, pl.ds(row, ROWS), :] = total_of(
                                [
                                    turned[jg][turn] * coef[mode, kg, jg, turn]
                                    for jg in range(groups)
                                    for turn in range(QUARTERS)
                                ]
                            )
            return carry

        lax.fori_loop(0, rows, mix_step, 0, unroll=UNROLL)

    def multiply_right(part):
        begin, rows = THERE[part]
        for mode in range(modes):
            shift = shift_ref[mode]
            upper_coef = occupation_ref[mode] + 1.0 - kind
            lower_coef = occupation_ref[mode] + kind
            for kg in range(groups):
                for height in range(heights):

                    def right_step(row, carry):
                        values = []
                        for col in range(ORB):
                            first = ((row * ORB + col) * 2 + 1) * n_energy + height * ROWS
                            upper = mixed[mode, kg, pl.ds(first + shift, ROWS), :]
                            lower = mixed[mode, kg, pl.ds(first - shift, ROWS), :]
                            values.append(upper_coef * upper + lower_coef * lower)
                        for n in range(ORB):
                            right_done[mode, kg, height, row * ORB + n] = total_of(
                                [
                                    values[col] * coupling[mode * PAIRS + n * ORB + col]
                                    for col in range(ORB)
                                ]
                            )
                        return carry

                    lax.fori_loop(
                        begin * QUARTERS // ORB,
                        (begin + rows) * QUARTERS // ORB,
                        right_step,
                        0,
                        unroll=2,
                    )

    def multiply_left(part):
        begin, rows = HOME[part]
        back = back_refs[part]
        for kg in range(groups):
            for height in range(heights):

                def left_step(n, carry):
                    values = [
                        [right_done[mode, kg, height, row * ORB + n] for row in range(ORB)]
                        for mode in range(modes)
                    ]
                    for i in range(begin * QUARTERS // ORB, (begin + rows) * QUARTERS // ORB):
                        both_done[kg, height, i * ORB + n] = total_of(
                            [
                                values[mode][row] * coupling[mode * PAIRS + i * ORB + row]
                                for mode in range(modes)
                                for row in range(ORB)
                            ]
                        )
                    return carry

                lax.fori_loop(0, ORB, left_step, 0, unroll=2)

        def unmix_step(step, carry):
            for kg in range(groups):
                for height in range(heights):
                    pair = QUARTERS * (begin + step)
                    values = [both_done[kg, height, pair + q] for q in range(QUARTERS)]
                    for kl, value in enumerate(swap_groups(values, lane, LANES // QUARTERS)):
                        row = ((kg * QUARTERS + kl) * n_energy + height * ROWS) * SLOT + step
                        back[pl.ds(row, ROWS, stride=SLOT), :] = value
            return carry

        lax.fori_loop(0, rows, unmix_step, 0, unroll=UNROLL)

    for part, (_, rows) in enumerate(THERE):
        own_there[part].wait()
        wait_all(arrived_refs[part], rows, recv_sem.at[part])
        mix(part)
        multiply_right(part)
    own_home = []
    for part in range(len(HOME)):
        multiply_left(part)
        own_home.append(start_home(part))
    for part, (_, rows) in enumerate(THERE):
        wait_all(packed_refs[part], rows, send_sem.at[part])

    def store_of(index, tile):
        return pltpu.make_async_copy(
            outside.at[tile, pl.ds(index * 2 * PAIRS, 2 * PAIRS)],
            out_ref.at[index, :, pl.ds(pl.multiple_of(tile * LANES, LANES), LANES)],
            local_sem.at[index, tile],
        )

    for part, (begin, rows) in enumerate(HOME):
        own_home[part].wait()
        wait_all(returned_refs[part], rows, recv_back_sem.at[part])

        def unpack(tile, carry):
            for place in range(0, rows, ROWS):
                values = []
                for g in range(PIECES):
                    row = slot_of_rank(tile * PIECES + g) + place
                    values.append(
                        returned_refs[part][pl.ds(pl.multiple_of(row, ROWS), ROWS), :]
                    )
                kept = min(ROWS, rows - place)
                for p, value in enumerate(swap_groups(values, lane, GROUP)):
                    first = piece_rows(p) + QUARTERS * (begin + place)
                    outside[tile, pl.ds(first, kept, stride=QUARTERS), :] = value[:kept]
            if part == len(HOME) - 1:
                for index in range(2):
                    store_of(index, tile).start()
            return carry

        lax.fori_loop(0, tiles, unpack, 0)

    for part, (_, rows) in enumerate(HOME):
        wait_all(back_refs[part], rows, send_back_sem.at[part])

    def finish(tile, carry):
        for index in range(2):
            store_of(index, tile).wait()
        return carry

    lax.fori_loop(0, tiles, finish, 0)


def on_device(green_blocks, couple_matrix, occupation, energy_shift, branch_weight, pair_branch):
    n_energy = lax.axis_size("energy")
    n_moment = lax.axis_size("momentum")
    modes = couple_matrix.shape[0]
    width, atoms = green_blocks.shape[3:]
    count = n_energy * n_moment
    tiles = atoms // LANES
    groups = n_moment // QUARTERS
    heights = n_energy // ROWS
    assert green_blocks.shape[1:3] == (1, 1) and width == 2 * PAIRS
    assert couple_matrix.shape[2] == GROUP
    slots = pltpu.VMEM((count * SLOT, LANES), jnp.float32)
    there_slots, home_slots = (slots,) * len(THERE), (slots,) * len(HOME)
    there_sems = pltpu.SemaphoreType.DMA((len(THERE),))
    home_sems = pltpu.SemaphoreType.DMA((len(HOME),))
    spare = QUARTERS * ROWS
    result = pl.pallas_call(
        functools.partial(kernel, n_energy, n_moment, modes),
        out_shape=pltpu.VMEM((2, width, atoms), jnp.float32),
        in_specs=[pl.BlockSpec(memory_space=pl.ANY)] * 6,
        out_specs=pl.BlockSpec(memory_space=pl.ANY),
        scratch_shapes=[
            pltpu.SMEM(energy_shift.shape, jnp.int32),
            pltpu.SMEM(occupation.shape, jnp.float32),
            pltpu.SMEM(branch_weight.shape, jnp.float32),
            pltpu.SMEM(pair_branch.shape, jnp.int32),
            pltpu.VMEM((modes, GROUP, PAIRS), jnp.float32),
            pltpu.VMEM((tiles, 2 * width + spare, LANES), jnp.float32),
            there_slots,
            there_slots,
            pltpu.VMEM((modes, groups, (2 * PAIRS + 1) * n_energy, LANES), jnp.float32),
            pltpu.VMEM((modes * PAIRS, ROWS, LANES), jnp.float32),
            pltpu.VMEM((modes, groups, groups, QUARTERS, ROWS, LANES), jnp.float32),
            pltpu.VMEM((modes, groups, heights, PAIRS, ROWS, LANES), jnp.float32),
            pltpu.VMEM((groups, heights, PAIRS, ROWS, LANES), jnp.float32),
            home_slots,
            home_slots,
            pltpu.VMEM((tiles, 2 * width, LANES), jnp.float32),
            pltpu.SemaphoreType.DMA((2, tiles)),
            pltpu.SemaphoreType.DMA((5,)),
            there_sems,
            there_sems,
            there_sems,
            home_sems,
            home_sems,
            home_sems,
        ],
        compiler_params=pltpu.CompilerParams(
            collective_id=0, has_side_effects=True, vmem_limit_bytes=60 * 1024 * 1024
        ),
        name="self_energy",
    )(
        energy_shift,
        occupation,
        branch_weight,
        pair_branch,
        couple_matrix.transpose(0, 2, 1),
        green_blocks.reshape(2, width, atoms),
    )
    return result.reshape(green_blocks.shape)


def solution(mesh):
    in_specs = (
        P(None, "energy", "momentum", None, None),
        P(None, None, ("energy", "momentum")),
        P(),
        P(),
        P(),
        P(),
    )
    out_specs = P(None, "energy", "momentum", None, None)
    return jax.shard_map(
        on_device, mesh=mesh, in_specs=in_specs, out_specs=out_specs, check_vma=False
    )
```

```python
import functools

import jax
import jax.numpy as jnp
from jax import lax
from jax.experimental import pallas as pl
from jax.experimental.pallas import tpu as pltpu
from jax.sharding import PartitionSpec as P

ORB = 10
PAIRS = ORB * ORB
LANES = 128
ROWS = 8
GROUP = 8
PIECES = LANES // GROUP
QUARTERS = 4
STEPS = PAIRS // QUARTERS
SLOT = 16
THERE = ((0, 10), (10, 10), (20, 5))
HOME = ((0, 5), (5, 15), (20, 5))
UNROLL = 5
MESH = pl.DeviceIdType.MESH


def swap_groups(arrays, lane, width):
    arrays = list(arrays)
    bit = 1
    while bit < len(arrays):
        low = ((lane // width) & bit) == 0
        for p in range(len(arrays)):
            if p & bit:
                continue
            a, b = arrays[p], arrays[p | bit]
            arrays[p] = jnp.where(low, a, pltpu.roll(b, bit * width, 1))
            arrays[p | bit] = jnp.where(low, pltpu.roll(a, LANES - bit * width, 1), b)
        bit *= 2
    return arrays


def total_of(terms):
    while len(terms) > 1:
        paired = [terms[i] + terms[i + 1] for i in range(0, len(terms) - 1, 2)]
        terms = paired + ([terms[-1]] if len(terms) % 2 else [])
    return terms[0]


def piece_rows(piece):
    quarter, kind, part = piece // 4, (piece // 2) % 2, piece % 2
    return kind * 2 * PAIRS + part * PAIRS + quarter


def kernel(
    n_energy,
    n_moment,
    modes,
    shift_hbm,
    occupation_hbm,
    weight_hbm,
    branch_hbm,
    couple_hbm,
    green_ref,
    out_ref,
    shift_ref,
    occupation_ref,
    weight_ref,
    branch_ref,
    couple_ref,
    inside,
    packed_refs,
    arrived_refs,
    mixed,
    coupling,
    coef,
    right_done,
    both_done,
    back_refs,
    returned_refs,
    outside,
    local_sem,
    small_sem,
    send_sem,
    recv_sem,
    own_sem,
    send_back_sem,
    recv_back_sem,
    own_back_sem,
):
    count = n_energy * n_moment
    tiles = green_ref.shape[2] // LANES
    groups = n_moment // QUARTERS
    heights = n_energy // ROWS
    my_energy = lax.axis_index("energy")
    my_moment = lax.axis_index("momentum")

    def slot_of(energy, moment):
        return pl.multiple_of((moment * n_energy + energy) * SLOT, SLOT)

    def slot_of_rank(rank):
        return slot_of(rank // n_moment, rank % n_moment)

    order = sorted(range(n_moment), key=lambda step: -min(step, n_moment - step))
    stride = n_energy // n_moment

    def for_partners(action):
        def ring(turn, carry, steps=tuple(order)):
            for step in steps:
                action(
                    lax.rem(my_energy + turn + stride * step, n_energy),
                    lax.rem(my_moment + step, n_moment),
                )
            return carry

        ring(0, 0, [step for step in order if step > 0])
        lax.fori_loop(1, n_energy, ring, 0)

    loads = []
    for kind in range(2):
        for tile in range(tiles):
            load = pltpu.make_async_copy(
                green_ref.at[kind, :, pl.ds(tile * LANES, LANES)],
                inside.at[tile, pl.ds(kind * 2 * PAIRS, 2 * PAIRS)],
                local_sem.at[kind, tile],
            )
            load.start()
            loads.append(load)

    small_loads = []
    for index, (source, target) in enumerate(
        (
            (couple_hbm, couple_ref),
            (shift_hbm, shift_ref),
            (occupation_hbm, occupation_ref),
            (weight_hbm, weight_ref),
            (branch_hbm, branch_ref),
        )
    ):
        load = pltpu.make_async_copy(source, target, small_sem.at[index])
        load.start()
        small_loads.append(load)

    barrier = pltpu.get_barrier_semaphore()

    def greet(energy, moment):
        pl.semaphore_signal(
            barrier, inc=1, device_id={"energy": energy, "momentum": moment}, device_id_type=MESH
        )

    for_partners(greet)

    lane = lax.broadcasted_iota(jnp.int32, (ROWS, LANES), 1)

    for load in loads:
        load.wait()

    mine = slot_of(my_energy, my_moment)

    def pack(part):
        begin, rows = THERE[part]

        def pack_tile(tile, carry):
            for place in range(0, rows, ROWS):
                pieces = [
                    inside[
                        tile,
                        pl.ds(piece_rows(p) + QUARTERS * (begin + place), ROWS, stride=QUARTERS),
                        :,
                    ]
                    for p in range(PIECES)
                ]
                for g, value in enumerate(swap_groups(pieces, lane, GROUP)):
                    row = slot_of_rank(tile * PIECES + g) + place
                    packed_refs[part][pl.ds(pl.multiple_of(row, ROWS), ROWS), :] = value
            return carry

        lax.fori_loop(0, tiles, pack_tile, 0)

    def exchange_start(source, target, rows, send, receive, own_sem):
        def start(energy, moment):
            pltpu.make_async_remote_copy(
                src_ref=source.at[pl.ds(slot_of(energy, moment), rows)],
                dst_ref=target.at[pl.ds(mine, rows)],
                send_sem=send,
                recv_sem=receive,
                device_id={"energy": energy, "momentum": moment},
                device_id_type=MESH,
            ).start()

        for_partners(start)
        own = pltpu.make_async_copy(
            source.at[pl.ds(mine, rows)], target.at[pl.ds(mine, rows)], own_sem
        )
        own.start()
        return own

    def wait_all(buffer, rows, semaphore):
        every = buffer.at[pl.ds(0, (count - 1) * rows)]
        pltpu.make_async_copy(every, every, semaphore).wait()

    def start_there(part):
        return exchange_start(
            packed_refs[part],
            arrived_refs[part],
            THERE[part][1],
            send_sem.at[part],
            recv_sem.at[part],
            own_sem.at[part],
        )

    def start_home(part):
        return exchange_start(
            back_refs[part],
            returned_refs[part],
            HOME[part][1],
            send_back_sem.at[part],
            recv_back_sem.at[part],
            own_back_sem.at[part],
        )

    own_there = []
    for part in range(len(THERE)):
        pack(part)
        if part == 0:
            pl.semaphore_wait(barrier, count - 1)
        own_there.append(start_there(part))

    for load in small_loads:
        load.wait()
    spread = (
        lax.broadcasted_iota(jnp.int32, (GROUP, LANES), 1) % GROUP
        == lax.broadcasted_iota(jnp.int32, (GROUP, LANES), 0)
    ).astype(jnp.float32)
    for mode in range(modes):
        wide = lax.dot_general(
            couple_ref[mode],
            spread,
            (((0,), (0,)), ((), ())),
            precision=lax.Precision.HIGHEST,
            preferred_element_type=jnp.float32,
        )
        coupling[pl.ds(mode * PAIRS, PAIRS)] = jnp.broadcast_to(
            wide[:, None, :], (PAIRS, ROWS, LANES)
        )

    lane_moment = lane // (LANES // QUARTERS)
    for mode in range(modes):
        for kg in range(groups):
            for jg in range(groups):
                for turn in range(QUARTERS):
                    value = jnp.zeros((ROWS, LANES), jnp.float32)
                    for kl in range(QUARTERS):
                        k = kg * QUARTERS + kl
                        j = jg * QUARTERS + (kl - turn) % QUARTERS
                        weight = weight_ref[branch_ref[k, j], mode] / n_moment
                        value = jnp.where(lane_moment == kl, weight, value)
                    coef[mode, kg, jg, turn] = value
    kind = ((lane // (2 * GROUP)) % 2).astype(jnp.float32)

    empty = jnp.zeros((n_energy, LANES), jnp.float32)
    for mode in range(modes):
        for kg in range(groups):

            def clear(pair, carry):
                row = pl.multiple_of(pair * 2 * n_energy, ROWS)
                mixed[mode, kg, pl.ds(row, n_energy), :] = empty
                return carry

            lax.fori_loop(0, PAIRS + 1, clear, 0, unroll=True)

    def mix(part):
        begin, rows = THERE[part]
        arrived = arrived_refs[part]

        def mix_step(step, carry):
            for height in range(heights):
                quarters = []
                for jg in range(groups):
                    values = [
                        arrived[
                            pl.ds(
                                ((jg * QUARTERS + jl) * n_energy + height * ROWS) * SLOT + step,
                                ROWS,
                                stride=SLOT,
                            ),
                            :,
                        ]
                        for jl in range(QUARTERS)
                    ]
                    quarters.append(swap_groups(values, lane, LANES // QUARTERS))
                for q in range(QUARTERS):
                    turned = [
                        [quarters[jg][q]]
                        + [
                            pltpu.roll(quarters[jg][q], turn * (LANES // QUARTERS), 1)
                            for turn in range(1, QUARTERS)
                        ]
                        for jg in range(groups)
                    ]
                    pair = QUARTERS * (begin + step) + q
                    row = pl.multiple_of((pair * 2 + 1) * n_energy + height * ROWS, ROWS)
                    for mode in range(modes):
                        for kg in range(groups):
                            mixed[mode, kg, pl.ds(row, ROWS), :] = total_of(
                                [
                                    turned[jg][turn] * coef[mode, kg, jg, turn]
                                    for jg in range(groups)
                                    for turn in range(QUARTERS)
                                ]
                            )
            return carry

        lax.fori_loop(0, rows, mix_step, 0, unroll=UNROLL)

    def multiply_right(part):
        begin, rows = THERE[part]
        for mode in range(modes):
            shift = shift_ref[mode]
            upper_coef = occupation_ref[mode] + 1.0 - kind
            lower_coef = occupation_ref[mode] + kind
            for kg in range(groups):
                for height in range(heights):

                    def right_step(row, carry):
                        values = []
                        for col in range(ORB):
                            first = ((row * ORB + col) * 2 + 1) * n_energy + height * ROWS
                            upper = mixed[mode, kg, pl.ds(first + shift, ROWS), :]
                            lower = mixed[mode, kg, pl.ds(first - shift, ROWS), :]
                            values.append(upper_coef * upper + lower_coef * lower)
                        for n in range(ORB):
                            right_done[mode, kg, height, row * ORB + n] = total_of(
                                [
                                    values[col] * coupling[mode * PAIRS + n * ORB + col]
                                    for col in range(ORB)
                                ]
                            )
                        return carry

                    lax.fori_loop(
                        begin * QUARTERS // ORB,
                        (begin + rows) * QUARTERS // ORB,
                        right_step,
                        0,
                        unroll=2,
                    )

    def multiply_left(part):
        begin, rows = HOME[part]
        back = back_refs[part]
        for kg in range(groups):
            for height in range(heights):

                def left_step(n, carry):
                    values = [
                        [right_done[mode, kg, height, row * ORB + n] for row in range(ORB)]
                        for mode in range(modes)
                    ]
                    for i in range(begin * QUARTERS // ORB, (begin + rows) * QUARTERS // ORB):
                        both_done[kg, height, i * ORB + n] = total_of(
                            [
                                values[mode][row] * coupling[mode * PAIRS + i * ORB + row]
                                for mode in range(modes)
                                for row in range(ORB)
                            ]
                        )
                    return carry

                lax.fori_loop(0, ORB, left_step, 0, unroll=2)

        def unmix_step(step, carry):
            for kg in range(groups):
                for height in range(heights):
                    pair = QUARTERS * (begin + step)
                    values = [both_done[kg, height, pair + q] for q in range(QUARTERS)]
                    for kl, value in enumerate(swap_groups(values, lane, LANES // QUARTERS)):
                        row = ((kg * QUARTERS + kl) * n_energy + height * ROWS) * SLOT + step
                        back[pl.ds(row, ROWS, stride=SLOT), :] = value
            return carry

        lax.fori_loop(0, rows, unmix_step, 0, unroll=UNROLL)

    for part, (_, rows) in enumerate(THERE):
        own_there[part].wait()
        wait_all(arrived_refs[part], rows, recv_sem.at[part])
        mix(part)
        multiply_right(part)
    own_home = []
    for part in range(len(HOME)):
        multiply_left(part)
        own_home.append(start_home(part))
    for part, (_, rows) in enumerate(THERE):
        wait_all(packed_refs[part], rows, send_sem.at[part])

    def store_of(index, tile):
        return pltpu.make_async_copy(
            outside.at[tile, pl.ds(index * 2 * PAIRS, 2 * PAIRS)],
            out_ref.at[index, :, pl.ds(pl.multiple_of(tile * LANES, LANES), LANES)],
            local_sem.at[index, tile],
        )

    for part, (begin, rows) in enumerate(HOME):
        own_home[part].wait()
        wait_all(returned_refs[part], rows, recv_back_sem.at[part])

        def unpack(tile, carry):
            for place in range(0, rows, ROWS):
                values = []
                for g in range(PIECES):
                    row = slot_of_rank(tile * PIECES + g) + place
                    values.append(
                        returned_refs[part][pl.ds(pl.multiple_of(row, ROWS), ROWS), :]
                    )
                kept = min(ROWS, rows - place)
                for p, value in enumerate(swap_groups(values, lane, GROUP)):
                    first = piece_rows(p) + QUARTERS * (begin + place)
                    outside[tile, pl.ds(first, kept, stride=QUARTERS), :] = value[:kept]
            if part == len(HOME) - 1:
                for index in range(2):
                    store_of(index, tile).start()
            return carry

        lax.fori_loop(0, tiles, unpack, 0)

    for part, (_, rows) in enumerate(HOME):
        wait_all(back_refs[part], rows, send_back_sem.at[part])

    def finish(tile, carry):
        for index in range(2):
            store_of(index, tile).wait()
        return carry

    lax.fori_loop(0, tiles, finish, 0)


def on_device(green_blocks, couple_matrix, occupation, energy_shift, branch_weight, pair_branch):
    n_energy = lax.axis_size("energy")
    n_moment = lax.axis_size("momentum")
    modes = couple_matrix.shape[0]
    width, atoms = green_blocks.shape[3:]
    count = n_energy * n_moment
    tiles = atoms // LANES
    groups = n_moment // QUARTERS
    heights = n_energy // ROWS
    assert green_blocks.shape[1:3] == (1, 1) and width == 2 * PAIRS
    assert couple_matrix.shape[2] == GROUP
    slots = pltpu.VMEM((count * SLOT, LANES), jnp.float32)
    there_slots, home_slots = (slots,) * len(THERE), (slots,) * len(HOME)
    there_sems = pltpu.SemaphoreType.DMA((len(THERE),))
    home_sems = pltpu.SemaphoreType.DMA((len(HOME),))
    spare = QUARTERS * ROWS
    result = pl.pallas_call(
        functools.partial(kernel, n_energy, n_moment, modes),
        out_shape=pltpu.VMEM((2, width, atoms), jnp.float32),
        in_specs=[pl.BlockSpec(memory_space=pl.ANY)] * 6,
        out_specs=pl.BlockSpec(memory_space=pl.ANY),
        scratch_shapes=[
            pltpu.SMEM(energy_shift.shape, jnp.int32),
            pltpu.SMEM(occupation.shape, jnp.float32),
            pltpu.SMEM(branch_weight.shape, jnp.float32),
            pltpu.SMEM(pair_branch.shape, jnp.int32),
            pltpu.VMEM((modes, GROUP, PAIRS), jnp.float32),
            pltpu.VMEM((tiles, 2 * width + spare, LANES), jnp.float32),
            there_slots,
            there_slots,
            pltpu.VMEM((modes, groups, (2 * PAIRS + 1) * n_energy, LANES), jnp.float32),
            pltpu.VMEM((modes * PAIRS, ROWS, LANES), jnp.float32),
            pltpu.VMEM((modes, groups, groups, QUARTERS, ROWS, LANES), jnp.float32),
            pltpu.VMEM((modes, groups, heights, PAIRS, ROWS, LANES), jnp.float32),
            pltpu.VMEM((groups, heights, PAIRS, ROWS, LANES), jnp.float32),
            home_slots,
            home_slots,
            pltpu.VMEM((tiles, 2 * width, LANES), jnp.float32),
            pltpu.SemaphoreType.DMA((2, tiles)),
            pltpu.SemaphoreType.DMA((5,)),
            there_sems,
            there_sems,
            there_sems,
            home_sems,
            home_sems,
            home_sems,
        ],
        compiler_params=pltpu.CompilerParams(
            collective_id=0, has_side_effects=True, vmem_limit_bytes=60 * 1024 * 1024
        ),
        name="self_energy",
    )(
        energy_shift,
        occupation,
        branch_weight,
        pair_branch,
        couple_matrix.transpose(0, 2, 1),
        green_blocks.reshape(2, width, atoms),
    )
    return result.reshape(green_blocks.shape)


def solution(mesh):
    in_specs = (
        P(None, "energy", "momentum", None, None),
        P(None, None, ("energy", "momentum")),
        P(),
        P(),
        P(),
        P(),
    )
    out_specs = P(None, "energy", "momentum", None, None)
    return jax.shard_map(
        on_device, mesh=mesh, in_specs=in_specs, out_specs=out_specs, check_vma=False
    )
```

```python
import functools

import jax
import jax.numpy as jnp
from jax import lax
from jax.experimental import pallas as pl
from jax.experimental.pallas import tpu as pltpu
from jax.sharding import PartitionSpec as P

ORB = 10
PAIRS = ORB * ORB
LANES = 128
ROWS = 8
GROUP = 8
PIECES = LANES // GROUP
QUARTERS = 4
STEPS = PAIRS // QUARTERS
SLOT = 16
THERE = ((0, 10), (10, 10), (20, 5))
HOME = ((0, 5), (5, 10), (15, 10))
UNROLL = 5
MESH = pl.DeviceIdType.MESH


def swap_groups(arrays, lane, width):
    arrays = list(arrays)
    bit = 1
    while bit < len(arrays):
        low = ((lane // width) & bit) == 0
        for p in range(len(arrays)):
            if p & bit:
                continue
            a, b = arrays[p], arrays[p | bit]
            arrays[p] = jnp.where(low, a, pltpu.roll(b, bit * width, 1))
            arrays[p | bit] = jnp.where(low, pltpu.roll(a, LANES - bit * width, 1), b)
        bit *= 2
    return arrays


def total_of(terms):
    while len(terms) > 1:
        paired = [terms[i] + terms[i + 1] for i in range(0, len(terms) - 1, 2)]
        terms = paired + ([terms[-1]] if len(terms) % 2 else [])
    return terms[0]


def piece_rows(piece):
    quarter, kind, part = piece // 4, (piece // 2) % 2, piece % 2
    return kind * 2 * PAIRS + part * PAIRS + quarter


def kernel(
    n_energy,
    n_moment,
    modes,
    shift_hbm,
    occupation_hbm,
    weight_hbm,
    branch_hbm,
    couple_hbm,
    green_ref,
    out_ref,
    shift_ref,
    occupation_ref,
    weight_ref,
    branch_ref,
    couple_ref,
    inside,
    packed_refs,
    arrived_refs,
    mixed,
    coupling,
    coef,
    right_done,
    both_done,
    back_refs,
    returned_refs,
    outside,
    local_sem,
    small_sem,
    send_sem,
    recv_sem,
    own_sem,
    send_back_sem,
    recv_back_sem,
    own_back_sem,
):
    count = n_energy * n_moment
    tiles = green_ref.shape[2] // LANES
    groups = n_moment // QUARTERS
    heights = n_energy // ROWS
    my_energy = lax.axis_index("energy")
    my_moment = lax.axis_index("momentum")

    def slot_of(energy, moment):
        return pl.multiple_of((moment * n_energy + energy) * SLOT, SLOT)

    def slot_of_rank(rank):
        return slot_of(rank // n_moment, rank % n_moment)

    order = sorted(range(n_moment), key=lambda step: -min(step, n_moment - step))

    def for_partners(action):
        def ring(turn, carry, steps=tuple(order)):
            for step in steps:
                action(
                    lax.rem(my_energy + turn, n_energy),
                    lax.rem(my_moment + step, n_moment),
                )
            return carry

        ring(0, 0, [step for step in order if step > 0])
        lax.fori_loop(1, n_energy, ring, 0)

    loads = []
    for kind in range(2):
        for tile in range(tiles):
            load = pltpu.make_async_copy(
                green_ref.at[kind, :, pl.ds(tile * LANES, LANES)],
                inside.at[tile, pl.ds(kind * 2 * PAIRS, 2 * PAIRS)],
                local_sem.at[kind, tile],
            )
            load.start()
            loads.append(load)

    small_loads = []
    for index, (source, target) in enumerate(
        (
            (couple_hbm, couple_ref),
            (shift_hbm, shift_ref),
            (occupation_hbm, occupation_ref),
            (weight_hbm, weight_ref),
            (branch_hbm, branch_ref),
        )
    ):
        load = pltpu.make_async_copy(source, target, small_sem.at[index])
        load.start()
        small_loads.append(load)

    barrier = pltpu.get_barrier_semaphore()

    def greet(energy, moment):
        pl.semaphore_signal(
            barrier, inc=1, device_id={"energy": energy, "momentum": moment}, device_id_type=MESH
        )

    for_partners(greet)

    lane = lax.broadcasted_iota(jnp.int32, (ROWS, LANES), 1)

    for load in loads:
        load.wait()

    mine = slot_of(my_energy, my_moment)

    def pack(part):
        begin, rows = THERE[part]

        def pack_tile(tile, carry):
            for place in range(0, rows, ROWS):
                pieces = [
                    inside[
                        tile,
                        pl.ds(piece_rows(p) + QUARTERS * (begin + place), ROWS, stride=QUARTERS),
                        :,
                    ]
                    for p in range(PIECES)
                ]
                for g, value in enumerate(swap_groups(pieces, lane, GROUP)):
                    row = slot_of_rank(tile * PIECES + g) + place
                    packed_refs[part][pl.ds(pl.multiple_of(row, ROWS), ROWS), :] = value
            return carry

        lax.fori_loop(0, tiles, pack_tile, 0)

    def exchange_start(source, target, rows, send, receive, own_sem):
        def start(energy, moment):
            pltpu.make_async_remote_copy(
                src_ref=source.at[pl.ds(slot_of(energy, moment), rows)],
                dst_ref=target.at[pl.ds(mine, rows)],
                send_sem=send,
                recv_sem=receive,
                device_id={"energy": energy, "momentum": moment},
                device_id_type=MESH,
            ).start()

        for_partners(start)
        own = pltpu.make_async_copy(
            source.at[pl.ds(mine, rows)], target.at[pl.ds(mine, rows)], own_sem
        )
        own.start()
        return own

    def wait_all(buffer, rows, semaphore):
        every = buffer.at[pl.ds(0, (count - 1) * rows)]
        pltpu.make_async_copy(every, every, semaphore).wait()

    def start_there(part):
        return exchange_start(
            packed_refs[part],
            arrived_refs[part],
            THERE[part][1],
            send_sem.at[part],
            recv_sem.at[part],
            own_sem.at[part],
        )

    def start_home(part):
        return exchange_start(
            back_refs[part],
            returned_refs[part],
            HOME[part][1],
            send_back_sem.at[part],
            recv_back_sem.at[part],
            own_back_sem.at[part],
        )

    own_there = []
    for part in range(len(THERE)):
        pack(part)
        if part == 0:
            pl.semaphore_wait(barrier, count - 1)
        own_there.append(start_there(part))

    for load in small_loads:
        load.wait()
    spread = (
        lax.broadcasted_iota(jnp.int32, (GROUP, LANES), 1) % GROUP
        == lax.broadcasted_iota(jnp.int32, (GROUP, LANES), 0)
    ).astype(jnp.float32)
    for mode in range(modes):
        wide = lax.dot_general(
            couple_ref[mode],
            spread,
            (((0,), (0,)), ((), ())),
            precision=lax.Precision.HIGHEST,
            preferred_element_type=jnp.float32,
        )
        coupling[pl.ds(mode * PAIRS, PAIRS)] = jnp.broadcast_to(
            wide[:, None, :], (PAIRS, ROWS, LANES)
        )

    lane_moment = lane // (LANES // QUARTERS)
    for mode in range(modes):
        for kg in range(groups):
            for jg in range(groups):
                for turn in range(QUARTERS):
                    value = jnp.zeros((ROWS, LANES), jnp.float32)
                    for kl in range(QUARTERS):
                        k = kg * QUARTERS + kl
                        j = jg * QUARTERS + (kl - turn) % QUARTERS
                        weight = weight_ref[branch_ref[k, j], mode] / n_moment
                        value = jnp.where(lane_moment == kl, weight, value)
                    coef[mode, kg, jg, turn] = value
    kind = ((lane // (2 * GROUP)) % 2).astype(jnp.float32)

    empty = jnp.zeros((n_energy, LANES), jnp.float32)
    for mode in range(modes):
        for kg in range(groups):

            def clear(pair, carry):
                row = pl.multiple_of(pair * 2 * n_energy, ROWS)
                mixed[mode, kg, pl.ds(row, n_energy), :] = empty
                return carry

            lax.fori_loop(0, PAIRS + 1, clear, 0, unroll=True)

    def mix(part):
        begin, rows = THERE[part]
        arrived = arrived_refs[part]

        def mix_step(step, carry):
            for height in range(heights):
                quarters = []
                for jg in range(groups):
                    values = [
                        arrived[
                            pl.ds(
                                ((jg * QUARTERS + jl) * n_energy + height * ROWS) * SLOT + step,
                                ROWS,
                                stride=SLOT,
                            ),
                            :,
                        ]
                        for jl in range(QUARTERS)
                    ]
                    quarters.append(swap_groups(values, lane, LANES // QUARTERS))
                for q in range(QUARTERS):
                    turned = [
                        [quarters[jg][q]]
                        + [
                            pltpu.roll(quarters[jg][q], turn * (LANES // QUARTERS), 1)
                            for turn in range(1, QUARTERS)
                        ]
                        for jg in range(groups)
                    ]
                    pair = QUARTERS * (begin + step) + q
                    row = pl.multiple_of((pair * 2 + 1) * n_energy + height * ROWS, ROWS)
                    for mode in range(modes):
                        for kg in range(groups):
                            mixed[mode, kg, pl.ds(row, ROWS), :] = total_of(
                                [
                                    turned[jg][turn] * coef[mode, kg, jg, turn]
                                    for jg in range(groups)
                                    for turn in range(QUARTERS)
                                ]
                            )
            return carry

        lax.fori_loop(0, rows, mix_step, 0, unroll=UNROLL)

    def multiply_right(part):
        begin, rows = THERE[part]
        for mode in range(modes):
            shift = shift_ref[mode]
            upper_coef = occupation_ref[mode] + 1.0 - kind
            lower_coef = occupation_ref[mode] + kind
            for kg in range(groups):
                for height in range(heights):

                    def right_step(row, carry):
                        values = []
                        for col in range(ORB):
                            first = ((row * ORB + col) * 2 + 1) * n_energy + height * ROWS
                            upper = mixed[mode, kg, pl.ds(first + shift, ROWS), :]
                            lower = mixed[mode, kg, pl.ds(first - shift, ROWS), :]
                            values.append(upper_coef * upper + lower_coef * lower)
                        for n in range(ORB):
                            right_done[mode, kg, height, row * ORB + n] = total_of(
                                [
                                    values[col] * coupling[mode * PAIRS + n * ORB + col]
                                    for col in range(ORB)
                                ]
                            )
                        return carry

                    lax.fori_loop(
                        begin * QUARTERS // ORB,
                        (begin + rows) * QUARTERS // ORB,
                        right_step,
                        0,
                        unroll=2,
                    )

    def sum_left(first, last, rows, add):
        for kg in range(groups):
            for height in range(heights):

                def left_step(n, carry):
                    values = [
                        [right_done[mode, kg, height, row * ORB + n] for row in rows]
                        for mode in range(modes)
                    ]
                    for i in range(first, last):
                        terms = [
                            values[mode][index] * coupling[mode * PAIRS + i * ORB + row]
                            for mode in range(modes)
                            for index, row in enumerate(rows)
                        ]
                        if add:
                            terms.append(both_done[kg, height, i * ORB + n])
                        both_done[kg, height, i * ORB + n] = total_of(terms)
                    return carry

                lax.fori_loop(0, ORB, left_step, 0, unroll=2)

    last_row = THERE[-1][0] * QUARTERS // ORB

    def multiply_left(part):
        begin, rows = HOME[part]
        back = back_refs[part]
        sum_left(
            begin * QUARTERS // ORB,
            (begin + rows) * QUARTERS // ORB,
            range(last_row, ORB),
            True,
        )

        def unmix_step(step, carry):
            for kg in range(groups):
                for height in range(heights):
                    pair = QUARTERS * (begin + step)
                    values = [both_done[kg, height, pair + q] for q in range(QUARTERS)]
                    for kl, value in enumerate(swap_groups(values, lane, LANES // QUARTERS)):
                        row = ((kg * QUARTERS + kl) * n_energy + height * ROWS) * SLOT + step
                        back[pl.ds(row, ROWS, stride=SLOT), :] = value
            return carry

        lax.fori_loop(0, rows, unmix_step, 0, unroll=UNROLL)

    for part, (_, rows) in enumerate(THERE):
        if part == len(THERE) - 1:
            sum_left(0, ORB, range(last_row), False)
        own_there[part].wait()
        wait_all(arrived_refs[part], rows, recv_sem.at[part])
        mix(part)
        multiply_right(part)
    own_home = []
    for part in range(len(HOME)):
        multiply_left(part)
        own_home.append(start_home(part))
    for part, (_, rows) in enumerate(THERE):
        wait_all(packed_refs[part], rows, send_sem.at[part])

    def store_of(index, tile):
        return pltpu.make_async_copy(
            outside.at[tile, pl.ds(index * 2 * PAIRS, 2 * PAIRS)],
            out_ref.at[index, :, pl.ds(pl.multiple_of(tile * LANES, LANES), LANES)],
            local_sem.at[index, tile],
        )

    for part, (begin, rows) in enumerate(HOME):
        own_home[part].wait()
        wait_all(returned_refs[part], rows, recv_back_sem.at[part])

        def unpack(tile, carry):
            for place in range(0, rows, ROWS):
                values = []
                for g in range(PIECES):
                    row = slot_of_rank(tile * PIECES + g) + place
                    values.append(
                        returned_refs[part][pl.ds(pl.multiple_of(row, ROWS), ROWS), :]
                    )
                kept = min(ROWS, rows - place)
                for p, value in enumerate(swap_groups(values, lane, GROUP)):
                    first = piece_rows(p) + QUARTERS * (begin + place)
                    outside[tile, pl.ds(first, kept, stride=QUARTERS), :] = value[:kept]
            if part == len(HOME) - 1:
                for index in range(2):
                    store_of(index, tile).start()
            return carry

        lax.fori_loop(0, tiles, unpack, 0)

    for part, (_, rows) in enumerate(HOME):
        wait_all(back_refs[part], rows, send_back_sem.at[part])

    def finish(tile, carry):
        for index in range(2):
            store_of(index, tile).wait()
        return carry

    lax.fori_loop(0, tiles, finish, 0)


def on_device(green_blocks, couple_matrix, occupation, energy_shift, branch_weight, pair_branch):
    n_energy = lax.axis_size("energy")
    n_moment = lax.axis_size("momentum")
    modes = couple_matrix.shape[0]
    width, atoms = green_blocks.shape[3:]
    count = n_energy * n_moment
    tiles = atoms // LANES
    groups = n_moment // QUARTERS
    heights = n_energy // ROWS
    assert green_blocks.shape[1:3] == (1, 1) and width == 2 * PAIRS
    assert couple_matrix.shape[2] == GROUP
    slots = pltpu.VMEM((count * SLOT, LANES), jnp.float32)
    there_slots, home_slots = (slots,) * len(THERE), (slots,) * len(HOME)
    there_sems = pltpu.SemaphoreType.DMA((len(THERE),))
    home_sems = pltpu.SemaphoreType.DMA((len(HOME),))
    spare = QUARTERS * ROWS
    result = pl.pallas_call(
        functools.partial(kernel, n_energy, n_moment, modes),
        out_shape=pltpu.VMEM((2, width, atoms), jnp.float32),
        in_specs=[pl.BlockSpec(memory_space=pl.ANY)] * 6,
        out_specs=pl.BlockSpec(memory_space=pl.ANY),
        scratch_shapes=[
            pltpu.SMEM(energy_shift.shape, jnp.int32),
            pltpu.SMEM(occupation.shape, jnp.float32),
            pltpu.SMEM(branch_weight.shape, jnp.float32),
            pltpu.SMEM(pair_branch.shape, jnp.int32),
            pltpu.VMEM((modes, GROUP, PAIRS), jnp.float32),
            pltpu.VMEM((tiles, 2 * width + spare, LANES), jnp.float32),
            there_slots,
            there_slots,
            pltpu.VMEM((modes, groups, (2 * PAIRS + 1) * n_energy, LANES), jnp.float32),
            pltpu.VMEM((modes * PAIRS, ROWS, LANES), jnp.float32),
            pltpu.VMEM((modes, groups, groups, QUARTERS, ROWS, LANES), jnp.float32),
            pltpu.VMEM((modes, groups, heights, PAIRS, ROWS, LANES), jnp.float32),
            pltpu.VMEM((groups, heights, PAIRS, ROWS, LANES), jnp.float32),
            home_slots,
            home_slots,
            pltpu.VMEM((tiles, 2 * width, LANES), jnp.float32),
            pltpu.SemaphoreType.DMA((2, tiles)),
            pltpu.SemaphoreType.DMA((5,)),
            there_sems,
            there_sems,
            there_sems,
            home_sems,
            home_sems,
            home_sems,
        ],
        compiler_params=pltpu.CompilerParams(
            collective_id=0, has_side_effects=True, vmem_limit_bytes=60 * 1024 * 1024
        ),
        name="self_energy",
    )(
        energy_shift,
        occupation,
        branch_weight,
        pair_branch,
        couple_matrix.transpose(0, 2, 1),
        green_blocks.reshape(2, width, atoms),
    )
    return result.reshape(green_blocks.shape)


def solution(mesh):
    in_specs = (
        P(None, "energy", "momentum", None, None),
        P(None, None, ("energy", "momentum")),
        P(),
        P(),
        P(),
        P(),
    )
    out_specs = P(None, "energy", "momentum", None, None)
    return jax.shard_map(
        on_device, mesh=mesh, in_specs=in_specs, out_specs=out_specs, check_vma=False
    )
```
